128 devices in a mesh: hst: 8 (over x, core), wide: 16 (over z, y).
Axes of the slice: x: 4, y: 4, z: 4, core: 2. Of those that a mesh axis runs over, the one named last changes fastest.
Arguments:
- dense_out: bfloat16 [32768, 128], P(('hst', 'wide')), may hold values from -6 to 6
- pooled: bfloat16 [32768, 8192], P(('hst', 'wide')), may hold values from -6 to 6
- dense_cot: bfloat16 [32768, 128], P(('hst', 'wide')), may hold values from -6 to 6
- pair_cot: bfloat16 [32768, 2080], P(('hst', 'wide')), may hold values from -0.75 to 0.75
- bag_ids: int32 [64, 8, 32768], P(None, None, ('hst', 'wide')), may hold values from 0 to 4095
- weights: float32 [64, 4096, 128], P('wide', 'hst'), may hold values from -3 to 3
- accum: float32 [64, 4096], P('wide', 'hst'), may hold values from 50 to 2000
Outputs:
- d_dense: bfloat16 [32768, 128], P(('hst', 'wide'))
- new_weights: float32 [64, 4096, 128], P('wide', 'hst')
- new_accum: float32 [64, 4096], P('wide', 'hst')
The draws below stay inside these ranges and needn't reach their ends.
Inputs may be any that keep to these rules, and one draw needn't show every extreme that they name: `bag_ids`: each id names a row of its table.
All inputs are finite; a program needn't handle non-finite values.
Results may differ from the reference program's by a relative error of at most 0.0059.
Values may be sent and summed in bfloat16 or wider, within the bound.
No kernel may reach another device: no remote copies, remote signals or barrier semaphores. Data moves between devices by JAX's collectives and lax.ppermute only.
A program may use at most 192 MiB of HBM per device.

```python
import math
import jax
import jax.numpy as jnp
import numpy as np
from jax import lax

E = 128
NT = 64
HOT = 8
BD = 256
FEAT = 65
PAIRS = 2080
ROWS = 4096
BATCH = 32768


def with_ends(array, stream_key, least, top_value):
    extent = array.shape
    place = [jax.random.randint(jax.random.fold_in(stream_key, axis), (), 0, extent[axis]) for axis in range(len(extent))]
    array = array.at[tuple(place)].set(least)
    longest = extent.index(max(extent))
    place[longest] = (place[longest] + 1) % extent[longest]
    return array.at[tuple(place)].set(top_value)


def level_of(key, extent, cuts, least, high):
    gain = 1.0
    for dim, shards_of in cuts:
        heights = jax.random.uniform(jax.random.fold_in(jax.random.fold_in(key, 6), dim), (shards_of,), jnp.float32, least / len(cuts), high / len(cuts))
        gain = gain * jnp.repeat(jnp.exp(heights), extent[dim] // shards_of).reshape((-1,) + (1,) * (len(extent) - 1 - dim))
    return gain


def cumulative_ranks(number_of, skew):
    portions = [(1 << 20) // math.isqrt(grade ** skew) + 1 for grade in range(1, number_of + 1)]
    width = 1 + sum(portions) // (1 << 30)
    return np.cumsum(np.array([max(1, weight // width) for weight in portions]))


def ranked_ids(own_key, dims, amount, lean):
    listing = cumulative_ranks(amount, lean)
    ticket = jax.random.randint(jax.random.fold_in(own_key, 1), dims, 0, int(listing[amount - 1]))
    rank = jnp.searchsorted(jnp.asarray(listing, jnp.int32), ticket, side="right")
    return jax.random.permutation(jax.random.fold_in(own_key, 2), amount)[rank].astype(jnp.int32)


def bell_draw(stream_key, extent, scale, limit, split=(), kind=jnp.bfloat16):
    loudness = level_of(stream_key, extent, split, -0.22, 0.18) if split else 1.0
    values = jax.random.normal(stream_key, extent, jnp.float32) * scale * loudness
    return jnp.minimum(jnp.maximum(values, -limit), limit).astype(kind)


def setup_inputs(seed: int = 0) -> dict:
    keys = jax.random.split(jax.random.key(seed), 8)
    dense_out = bell_draw(keys[0], (BATCH, E), 1.0, 6.0, ((0, 128),))
    pooled = bell_draw(keys[1], (BATCH, NT * E), 1.0, 6.0, ((0, 128),))
    dense_cot = bell_draw(keys[2], (BATCH, E), 1.0, 6.0, ((0, 128),))
    pair_cot = bell_draw(keys[3], (BATCH, PAIRS), 0.125, 0.75, ((0, 128),))
    bag_ids = with_ends(ranked_ids(keys[4], (NT, HOT, BATCH), ROWS, 2), jax.random.fold_in(keys[4], 3), 0, ROWS - 1).astype(jnp.int32)
    weights = bell_draw(keys[5], (NT, ROWS, E), 0.5, 3.0, ((0, 16), (1, 8)), jnp.float32)
    accum = jnp.clip(jnp.exp(math.log(2000.0) - 3.6888795 * jax.random.uniform(keys[6], (NT, ROWS), jnp.float32) ** level_of(keys[6], (NT, ROWS), ((0, 16), (1, 8)), -0.2, 0.2)), 50.0, 2000.0)
    return dict(dense_out=dense_out, pooled=pooled, dense_cot=dense_cot, pair_cot=pair_cot, bag_ids=bag_ids, weights=weights, accum=accum)


LEARN_RATE = 0.5
EPSILON = 1e-08

def pair_slots():
    column = np.arange(FEAT * FEAT)
    first = column // FEAT
    second = column % FEAT
    upper = np.maximum(first, second)
    lower = np.minimum(first, second)
    slots = upper * (upper - 1) // 2 + lower
    return np.where(first == second, PAIRS, slots).astype(np.int32)

def table_rows(grads_table, ids_table):
    spread = jnp.broadcast_to(grads_table[None], (HOT, BD, E)).reshape(HOT * BD, E)
    return jax.ops.segment_sum(spread, ids_table.reshape(-1), num_segments=ROWS)

def reference(dense_out, pooled, dense_cot, pair_cot, bag_ids, weights, accum):
    slots = jnp.asarray(pair_slots())
    blocks = dense_out.shape[0] // BD

    def block_step(totals, number):
        offset = number * BD
        dense_part = lax.dynamic_slice_in_dim(dense_out, offset, BD, 0)
        pooled_part = lax.dynamic_slice_in_dim(pooled, offset, BD, 0).reshape(BD, NT, E)
        cot_part = lax.dynamic_slice_in_dim(dense_cot, offset, BD, 0)
        pair_part = lax.dynamic_slice_in_dim(pair_cot, offset, BD, 0)
        ids_part = lax.dynamic_slice_in_dim(bag_ids, offset, BD, 2)
        features = jnp.concatenate([dense_part[:, None, :], pooled_part], 1).astype(jnp.float32)
        padded = jnp.concatenate([pair_part, jnp.zeros((BD, 1), jnp.bfloat16)], 1)
        pair_grad = jnp.take(padded, slots, axis=1).reshape(BD, FEAT, FEAT).astype(jnp.float32)
        feat_grads = jnp.einsum('bij,bje->bie', pair_grad, features)
        dense_grad = (feat_grads[:, 0] + cot_part.astype(jnp.float32)).astype(jnp.bfloat16)
        bag_grads = lax.optimization_barrier(feat_grads[:, 1:].astype(jnp.bfloat16)).astype(jnp.float32)
        rows = jax.vmap(table_rows)(bag_grads.transpose(1, 0, 2), ids_part)
        return (totals + rows, dense_grad)
    start_rows = jnp.zeros((NT, ROWS, E), jnp.float32)
    row_grads, dense_blocks = lax.scan(block_step, start_rows, jnp.arange(blocks, dtype=jnp.int32))
    d_dense = dense_blocks.reshape(blocks * BD, E)
    new_accum = accum + lax.optimization_barrier(jnp.mean(row_grads * row_grads, -1))
    new_weights = weights - LEARN_RATE * row_grads / (jnp.sqrt(new_accum)[..., None] + EPSILON)
    return (d_dense, new_weights, new_accum)
```

```python
import functools

import jax
import jax.numpy as jnp
from jax import lax
from jax.experimental import pallas as pl
from jax.experimental.pallas import tpu as pltpu
from jax.sharding import PartitionSpec as P

LEARN_RATE = 0.5
EPSILON = 1e-08
LANES = 128
HALF = 64
FIELD = 4
VMEM = 48 << 20
SEND_CHUNKS = ((0, 1, 2, 3),)
SUM_CHUNKS = ((0, 1), (2, 3))
BF16 = jnp.bfloat16
F32 = jnp.float32


def cost(micros):
    return pl.CostEstimate(flops=int(micros * 1.15e9), bytes_accessed=1 << 20, transcendentals=0)


def params():
    return pltpu.CompilerParams(vmem_limit_bytes=VMEM)


def interact_kernel(
    chunks, dense_ref, pooled_ref, cot_ref, pair_ref, d_dense_ref, *rest
):
    send_refs = rest[: len(chunks)]
    wide_pairs, lower, feats, grads = rest[len(chunks) :]
    block = dense_ref.shape[0]
    half = block // 2
    tables = pooled_ref.shape[1] // LANES
    per_owner = sum(len(chunk) for chunk in chunks)
    rows = lower.shape[1]

    @pl.when(pl.program_id(0) == 0)
    def _():
        lower[...] = jnp.zeros_like(lower)
        feats[...] = jnp.zeros_like(feats)

    wide_pairs[:, 0 : pair_ref.shape[1]] = pair_ref[...].astype(F32)
    lane = lax.broadcasted_iota(jnp.int32, (half, LANES), 1)
    for i in range(1, tables + 1):
        start = i * (i - 1) // 2
        base = start // LANES * LANES
        shift = start - base
        to_low = (LANES - shift) % LANES
        to_high = (HALF - shift) % LANES

        def rolled(first, amount, at):
            piece = wide_pairs[first : first + half, at : at + LANES]
            return pltpu.roll(piece, amount, 1) if amount else piece

        low = rolled(0, to_low, base)
        high = rolled(half, to_high, base)
        if shift + i > LANES:
            low = jnp.where(lane < LANES - shift, low, rolled(0, to_low, base + LANES))
            high = jnp.where(
                lane < HALF + LANES - shift, high, rolled(half, to_high, base + LANES)
            )
        if i < HALF:
            low = jnp.where(lane < i, low, 0.0)
            high = jnp.where(lane < HALF + i, high, 0.0)
        lower[:, i, :] = jnp.where(lane < HALF, low, high)

    feats[:, 0, :] = dense_ref[...].astype(F32)
    for t in range(tables):
        feats[:, t + 1, :] = pooled_ref[:, t * LANES : (t + 1) * LANES].astype(F32)

    row_lane = lax.broadcasted_iota(jnp.int32, (rows, LANES), 1)
    below = jnp.zeros((rows - HALF, LANES), F32)

    def two_samples(b, carry):
        both = lower[b]
        turned = jnp.concatenate([both.T, jnp.zeros((LANES, LANES - rows), F32)], 1)
        first = jnp.where(row_lane < HALF, both, 0.0)
        second = jnp.where(row_lane < HALF, pltpu.roll(both, HALF, 1), 0.0)
        first = first + jnp.concatenate([turned[:HALF], below], 0)
        second = second + jnp.concatenate([turned[HALF:], below], 0)
        for pairs, sample in ((first, b), (second, b + half)):
            out = jnp.dot(
                pairs[:, :rows].astype(BF16),
                feats[sample].astype(BF16),
                preferred_element_type=F32,
            )
            grads[:, pl.ds(sample, 1), :] = out.reshape(rows, 1, LANES)
        return carry

    lax.fori_loop(0, half, two_samples, 0, unroll=8)

    d_dense_ref[...] = (grads[0, 0:block] + cot_ref[...].astype(F32)).astype(BF16)
    for send_ref, chunk in zip(send_refs, chunks):
        for place, t in enumerate(chunk):
            for owner in range(tables // per_owner):
                send_ref[owner, :, place * LANES : (place + 1) * LANES] = grads[
                    owner * per_owner + t + 1, 0:block
                ].astype(BF16)


def interact(dense_out, pooled, dense_cot, pair_cot, owners, chunks):
    samples = dense_out.shape[0]
    tables = pooled.shape[1] // LANES
    pairs = pair_cot.shape[1]
    block = 64
    rows = (tables + 1 + 7) // 8 * 8
    padded = (pairs // LANES + 1) * LANES
    return pl.pallas_call(
        functools.partial(interact_kernel, chunks),
        grid=(samples // block,),
        in_specs=[
            pl.BlockSpec((block, LANES), lambda s: (s, 0)),
            pl.BlockSpec((block, tables * LANES), lambda s: (s, 0)),
            pl.BlockSpec((block, LANES), lambda s: (s, 0)),
            pl.BlockSpec((block, pairs), lambda s: (s, 0)),
        ],
        out_specs=[pl.BlockSpec((block, LANES), lambda s: (s, 0))]
        + [
            pl.BlockSpec((owners, block, len(chunk) * LANES), lambda s: (0, s, 0))
            for chunk in chunks
        ],
        out_shape=[jax.ShapeDtypeStruct((samples, LANES), BF16)]
        + [
            jax.ShapeDtypeStruct((owners, samples, len(chunk) * LANES), BF16) for chunk in chunks
        ],
        scratch_shapes=[
            pltpu.VMEM((block, padded), F32),
            pltpu.VMEM((block // 2, rows, LANES), F32),
            pltpu.VMEM((block, rows, LANES), F32),
            pltpu.VMEM((rows, block + 8, LANES), F32),
        ],
        compiler_params=params(),
        cost_estimate=cost(25),
    )(dense_out, pooled, dense_cot, pair_cot)


def count_kernel(ids_ref, out_ref):
    sources, _, slots, samples = ids_ref.shape
    words = out_ref.shape[1]
    step = 64

    @pl.loop(0, sources)
    def _(source):
        ids = ids_ref[source, 0]
        word = ids & (words - 1)
        one = jnp.left_shift(1, FIELD * (ids // words))
        columns = pl.ds(pl.multiple_of(source * samples, samples), samples)

        @pl.loop(0, words // step)
        def _(part):
            start = pl.multiple_of(part * step, step)
            place = lax.broadcasted_iota(jnp.int32, (step, samples), 0) + start
            total = jnp.zeros((step, samples), jnp.int32)
            for slot in range(slots):
                total = total + jnp.where(
                    word[slot : slot + 1] == place, one[slot : slot + 1], 0
                )
            out_ref[0, pl.ds(start, step), columns] = total


def bag_counts(ids, words):
    sources, tables, slots, samples = ids.shape
    return pl.pallas_call(
        count_kernel,
        grid=(tables,),
        in_specs=[pl.BlockSpec((sources, 1, slots, samples), lambda t: (0, t, 0, 0))],
        out_specs=pl.BlockSpec((1, words, sources * samples), lambda t: (t, 0, 0)),
        out_shape=jax.ShapeDtypeStruct((tables, words, sources * samples), jnp.int32),
        compiler_params=params(),
        cost_estimate=cost(35),
    )(ids)


def sum_kernel(hst_ref, counts_ref, grads_ref, out_ref, total):
    samples = counts_ref.shape[2]
    cores, _, chips = out_ref.shape[:3]
    step = 1024
    here, core = hst_ref[0] // cores, lax.rem(hst_ref[0], cores)
    for at in range(0, samples, step):
        grads = grads_ref[at : at + step, :]
        counts = counts_ref[0, :, at : at + step]
        for c in range(cores):
            for d in range(chips):
                field = cores * lax.rem(here + d, chips) + lax.rem(core + c, cores)
                picked = (counts >> (FIELD * field)) & ((1 << FIELD) - 1)
                part = jnp.dot(
                    picked.astype(F32).astype(BF16), grads, preferred_element_type=F32
                )
                if at == 0:
                    total[c, d] = part
                else:
                    total[c, d] += part
    for c in range(cores):
        for d in range(chips):
            out_ref[c, 0, d] = total[c, d].astype(BF16)


def row_sums(hst, counts, grads, chunk, columns, cores):
    _, words, samples = counts.shape
    step = 256
    chips = 32 // FIELD // cores
    first, column = chunk[0], columns[0]
    return pl.pallas_call(
        sum_kernel,
        grid_spec=pltpu.PrefetchScalarGridSpec(
            num_scalar_prefetch=1,
            grid=(len(chunk), words // step),
            in_specs=[
                pl.BlockSpec((1, step, samples), lambda t, w, hst: (first + t, w, 0)),
                pl.BlockSpec((samples, LANES), lambda t, w, hst: (0, column + t)),
            ],
            out_specs=pl.BlockSpec(
                (cores, 1, chips, step, LANES), lambda t, w, hst: (0, t, 0, w, 0)
            ),
            scratch_shapes=[pltpu.VMEM((cores, chips, step, LANES), F32)],
        ),
        out_shape=jax.ShapeDtypeStruct((cores, len(chunk), chips, words, LANES), BF16),
        compiler_params=params(),
        cost_estimate=cost(11 * len(chunk)),
    )(hst, counts, grads)


def add_kernel(mine_ref, other_ref, *out_refs):
    for d, out_ref in enumerate(out_refs):
        out_ref[0] = (mine_ref[0, 0, d].astype(F32) + other_ref[0, d].astype(F32)).astype(BF16)


def exchange(sums, cores):
    _, tables, chips, words, lanes = sums.shape
    devices = cores * chips
    got = lax.ppermute(sums[1], "hst", [(i, i ^ 1) for i in range(devices)])
    pieces = pl.pallas_call(
        add_kernel,
        grid=(tables,),
        in_specs=[
            pl.BlockSpec((1, 1, chips, words, lanes), lambda t: (0, t, 0, 0, 0)),
            pl.BlockSpec((1, chips, words, lanes), lambda t: (t, 0, 0, 0)),
        ],
        out_specs=[pl.BlockSpec((1, words, lanes), lambda t: (t, 0, 0))] * chips,
        out_shape=[jax.ShapeDtypeStruct((tables, words, lanes), BF16)] * chips,
        compiler_params=params(),
        cost_estimate=cost(1.5),
    )(sums, got)
    out = [pieces[0]]
    for d in range(1, chips):
        ring = [(i, (i + cores * d) % devices) for i in range(devices)]
        out.append(lax.ppermute(pieces[d], "hst", ring))
    return out


def update_kernel(weights_ref, accum_ref, *rest):
    *grad_refs, new_weights_ref, new_accum_ref = rest
    words, lanes = weights_ref.shape[1:]
    grads = grad_refs[0][0].astype(F32)
    for grad_ref in grad_refs[1:]:
        grads = grads + grad_ref[0].astype(F32)
    mean = jnp.sum(grads * grads, 1, keepdims=True) * (1.0 / lanes)
    accum = jnp.broadcast_to(accum_ref[0], (lanes, words)).T + mean
    new_weights_ref[0] = weights_ref[0] - LEARN_RATE * grads / (jnp.sqrt(accum) + EPSILON)
    new_accum_ref[0] = accum.T[0:1]


def update(weights, accum, grads, chunk):
    tables, words, lanes = weights.shape
    first = chunk[0]
    here = pl.BlockSpec((1, words, lanes), lambda t: (first + t, 0, 0))
    part = pl.BlockSpec((1, words, lanes), lambda t: (t, 0, 0))
    return pl.pallas_call(
        update_kernel,
        grid=(len(chunk),),
        in_specs=[here, pl.BlockSpec((1, 1, words), lambda t: (first + t, 0, 0))]
        + [part] * len(grads),
        out_specs=[part, pl.BlockSpec((1, 1, words), lambda t: (t, 0, 0))],
        out_shape=[
            jax.ShapeDtypeStruct((len(chunk), words, lanes), F32),
            jax.ShapeDtypeStruct((len(chunk), 1, words), F32),
        ],
        compiler_params=params(),
        cost_estimate=cost(2),
    )(weights, accum.reshape(tables, 1, words), *grads)


def local(dense_out, pooled, dense_cot, pair_cot, bag_ids, weights, accum):
    samples = dense_out.shape[0]
    slots = bag_ids.shape[1]
    per_owner, words, _ = weights.shape
    owners = lax.axis_size("wide")
    cores = 2
    hst = lax.axis_index("hst").reshape(1)
    ids = bag_ids.reshape(owners, per_owner, slots, samples)
    ids = lax.all_to_all(ids, "wide", split_axis=0, concat_axis=0, tiled=True)
    d_dense, *sends = interact(dense_out, pooled, dense_cot, pair_cot, owners, SEND_CHUNKS)
    counts = bag_counts(ids, words)
    received = [
        lax.all_to_all(send, "wide", split_axis=0, concat_axis=0, tiled=True).reshape(
            owners * samples, -1
        )
        for send in sends
    ]
    weights_out, accum_out = [], []
    for chunk in SUM_CHUNKS:
        for number, carried in enumerate(SEND_CHUNKS):
            if chunk[0] in carried:
                columns = [carried.index(t) for t in chunk]
                sums = row_sums(hst, counts, received[number], chunk, columns, cores)
        w, a = update(weights, accum, exchange(sums, cores), chunk)
        weights_out.append(w)
        accum_out.append(a)
    new_weights = jnp.concatenate(weights_out, 0)
    new_accum = jnp.concatenate(accum_out, 0).reshape(per_owner, words)
    return d_dense, new_weights, new_accum


def solution(mesh):
    in_specs = (
        P(("hst", "wide"), None),
        P(("hst", "wide"), None),
        P(("hst", "wide"), None),
        P(("hst", "wide"), None),
        P(None, None, ("hst", "wide")),
        P("wide", "hst", None),
        P("wide", "hst"),
    )
    out_specs = (P(("hst", "wide"), None), P("wide", "hst", None), P("wide", "hst"))
    return jax.shard_map(local, mesh=mesh, in_specs=in_specs, out_specs=out_specs, check_vma=False)
```

```python
import functools

import jax
import jax.numpy as jnp
from jax import lax
from jax.experimental import pallas as pl
from jax.experimental.pallas import tpu as pltpu
from jax.sharding import Mesh
from jax.sharding import PartitionSpec as P

LEARN_RATE = 0.5
EPSILON = 1e-08
LANES = 128
HALF = 64
FIELD = 4
BLOCK = 32
CORES = 2
CODE = 7
VMEM = 62 << 20
SMALL = 12 << 20
EARLY = 64
LATE_GROUP = 8
BF16 = jnp.bfloat16
F32 = jnp.float32


def cost(micros):
    return pl.CostEstimate(flops=int(micros * 2e8), bytes_accessed=1 << 16, transcendentals=0)


def params(size=VMEM):
    return pltpu.CompilerParams(vmem_limit_bytes=size)


def encode(ids):
    high = lax.shift_right_logical(ids, CODE)
    value = ((1 << CODE) + (ids & ((1 << CODE) - 1))).astype(F32)
    for bit in range(5):
        value = jnp.where((high >> bit) & 1 == 1, value * 2.0 ** (1 << bit), value)
    return value.astype(BF16)


def decode(codes):
    value = codes.astype(F32)
    high = jnp.zeros(value.shape, jnp.int32)
    for bit in range(4, -1, -1):
        large = value >= 2.0 ** (CODE + (1 << bit))
        value = jnp.where(large, value * 2.0 ** -(1 << bit), value)
        high = jnp.where(large, high + (1 << bit), high)
    return (high << CODE) + value.astype(jnp.int32) - (1 << CODE)


def interact_kernel(steps, with_ids, dense_ref, pooled_ref, cot_ref, pair_ref, *rest):
    if with_ids:
        ids_ref, *rest = rest
    d_dense_ref, send_ref, *scratch = rest
    tables = pooled_ref.shape[1] // LANES
    held = tables // send_ref.shape[0]

    @pl.when(pl.program_id(0) == 0)
    def _():
        for ref in scratch[1:3]:
            ref[...] = jnp.zeros_like(ref)

    if not with_ids:
        interact_block(dense_ref, pooled_ref, cot_ref, pair_ref, d_dense_ref, send_ref, *scratch)
        return

    @pl.when(pl.program_id(0) < steps)
    def _():
        interact_block(dense_ref, pooled_ref, cot_ref, pair_ref, d_dense_ref, send_ref, *scratch)

    @pl.when(pl.program_id(0) == steps)
    def _():
        slots = ids_ref.shape[1]
        for owner in range(tables // held):
            ids = ids_ref[owner * held : (owner + 1) * held]
            send_ref[owner, 0 : held * slots, :] = encode(ids.reshape(held * slots, -1))


def interact_block(
    dense_ref, pooled_ref, cot_ref, pair_ref, d_dense_ref, send_ref, wide_pairs, lower, feats, grads
):
    block = dense_ref.shape[0]
    half = block // 2
    tables = pooled_ref.shape[1] // LANES
    rows = lower.shape[1]

    wide_pairs[:, 0 : pair_ref.shape[1]] = pair_ref[...].astype(F32)
    lane = lax.broadcasted_iota(jnp.int32, (half, LANES), 1)
    for i in range(1, tables + 1):
        start = i * (i - 1) // 2
        base = start // LANES * LANES
        shift = start - base
        to_low = (LANES - shift) % LANES
        to_high = (HALF - shift) % LANES

        def rolled(first, amount, at):
            piece = wide_pairs[first : first + half, at : at + LANES]
            return pltpu.roll(piece, amount, 1) if amount else piece

        low = rolled(0, to_low, base)
        high = rolled(half, to_high, base)
        if shift + i > LANES:
            low = jnp.where(lane < LANES - shift, low, rolled(0, to_low, base + LANES))
            high = jnp.where(
                lane < HALF + LANES - shift, high, rolled(half, to_high, base + LANES)
            )
        if i < HALF:
            low = jnp.where(lane < i, low, 0.0)
            high = jnp.where(lane < HALF + i, high, 0.0)
        lower[:, i, :] = jnp.where(lane < HALF, low, high)

    feats[:, 0, :] = dense_ref[...].astype(F32)
    for t in range(tables):
        feats[:, t + 1, :] = pooled_ref[:, t * LANES : (t + 1) * LANES].astype(F32)

    row_lane = lax.broadcasted_iota(jnp.int32, (rows, LANES), 1)
    below = jnp.zeros((rows - HALF, LANES), F32)

    def two_samples(b, carry):
        both = lower[b]
        turned = jnp.concatenate([both.T, jnp.zeros((LANES, LANES - rows), F32)], 1)
        first = jnp.where(row_lane < HALF, both, 0.0)
        second = jnp.where(row_lane < HALF, pltpu.roll(both, HALF, 1), 0.0)
        first = first + jnp.concatenate([turned[:HALF], below], 0)
        second = second + jnp.concatenate([turned[HALF:], below], 0)
        for pairs, sample in ((first, b), (second, b + half)):
            out = jnp.dot(
                pairs[:, :rows].astype(BF16),
                feats[sample].astype(BF16),
                preferred_element_type=F32,
            )
            grads[:, pl.ds(sample, 1), :] = out.reshape(rows, 1, LANES)
        return carry

    lax.fori_loop(0, half, two_samples, 0, unroll=8)

    d_dense_ref[...] = (grads[0, 0:block] + cot_ref[...].astype(F32)).astype(BF16)
    owners = send_ref.shape[0]
    held = tables // owners
    for t in range(tables):
        place = t % held * LANES
        send_ref[t // held, :, place : place + LANES] = grads[t + 1, 0:block].astype(BF16)


def interact(dense_out, pooled, dense_cot, pair_cot, ids, owners, first, samples):
    tables = pooled.shape[1] // LANES
    pairs = pair_cot.shape[1]
    held = tables // owners
    rows = (tables + 1 + 7) // 8 * 8
    padded = (pairs // LANES + 1) * LANES
    skip, steps = first // BLOCK, samples // BLOCK
    with_ids = ids is not None
    slots = ids.shape[1] if with_ids else 0

    def at(s):
        return (skip + jnp.minimum(s, steps - 1), 0)

    specs = [
        pl.BlockSpec((BLOCK, LANES), at),
        pl.BlockSpec((BLOCK, tables * LANES), at),
        pl.BlockSpec((BLOCK, LANES), at),
        pl.BlockSpec((BLOCK, pairs), at),
    ]
    operands = [dense_out, pooled, dense_cot, pair_cot]
    if with_ids:
        specs.append(pl.BlockSpec(ids.shape, lambda s: (0, 0, 0)))
        operands.append(ids)
    extra = 1 if with_ids else 0
    return pl.pallas_call(
        functools.partial(interact_kernel, steps, with_ids),
        grid=(steps + extra,),
        in_specs=specs,
        out_specs=[
            pl.BlockSpec((BLOCK, LANES), lambda s: (jnp.minimum(s, steps - 1), 0)),
            pl.BlockSpec((owners, BLOCK, held * LANES), lambda s: (0, s, 0)),
        ],
        out_shape=[
            jax.ShapeDtypeStruct((samples, LANES), BF16),
            jax.ShapeDtypeStruct((owners, samples + extra * held * slots, held * LANES), BF16),
        ],
        scratch_shapes=[
            pltpu.VMEM((BLOCK, padded), F32),
            pltpu.VMEM((BLOCK // 2, rows, LANES), F32),
            pltpu.VMEM((BLOCK, rows, LANES), F32),
            pltpu.VMEM((rows, BLOCK + 8, LANES), F32),
        ],
        compiler_params=params(),
        cost_estimate=cost(20 * samples / 256),
    )(*operands)


def count_kernel(first, samples, codes_ref, out_ref):
    sources, rows, _ = codes_ref.shape
    words, columns = out_ref.shape[2:]
    slots = 32 // FIELD
    bits = words.bit_length() - 1
    strip = 64
    table = pl.program_id(0)
    codes = jnp.concatenate(
        [codes_ref[source, :, first : first + samples] for source in range(sources)], 1
    ).astype(F32)
    mine = codes[:slots]
    for other in range(1, rows // slots):
        mine = jnp.where(table == other, codes[other * slots : (other + 1) * slots], mine)
    ids = decode(mine)
    word = ids & (words - 1)
    one = jnp.left_shift(1, FIELD * lax.shift_right_logical(ids, bits))
    total = one
    for by in range(1, slots):
        total = total + jnp.where(word == pltpu.roll(word, by, 0), pltpu.roll(one, by, 0), 0)
    place = lax.broadcasted_iota(jnp.int32, (strip, LANES), 0)
    for at in range(0, columns, LANES):
        words_at = [word[slot : slot + 1, at : at + LANES] for slot in range(slots)]
        totals_at = [total[slot : slot + 1, at : at + LANES] for slot in range(slots)]
        for start in range(0, words, strip):
            out = jnp.zeros((strip, LANES), jnp.int32)
            for slot in range(slots):
                out = jnp.where(words_at[slot] == place + start, totals_at[slot], out)
            out_ref[0, 0, start : start + strip, at : at + LANES] = out


def bag_counts(received, held, slots, words, first, samples, group):
    sources, rows, lanes = received.shape
    last = rows // (held * slots) - 1
    return pl.pallas_call(
        functools.partial(count_kernel, first, samples),
        grid=(held, sources // group),
        in_specs=[pl.BlockSpec((group, held * slots, lanes), lambda t, g: (g, last, 0))],
        out_specs=pl.BlockSpec((1, 1, words, group * samples), lambda t, g: (t, g, 0, 0)),
        out_shape=jax.ShapeDtypeStruct(
            (held, sources // group, words, group * samples), jnp.int32
        ),
        compiler_params=params(),
        cost_estimate=cost(24 * samples / 256),
    )(received)


def sum_kernel(plan, first, hst_ref, counts_ref, grads_ref, *rest):
    befores = () if first else rest[: len(plan)]
    outs = rest[0 if first else len(plan) :]
    totals = outs if first else outs[-len(plan) :]
    chips = 32 // FIELD // CORES
    here, core = hst_ref[0] // CORES, lax.rem(hst_ref[0], CORES)

    @pl.when(pl.program_id(1) == 0)
    def _():
        for number, total in enumerate(totals):
            total[...] = jnp.zeros_like(total) if first else befores[number][...]

    group, samples, _ = grads_ref.shape
    grads = grads_ref[...].reshape(group * samples, LANES)
    counts = counts_ref[0, 0]
    for number, ds in enumerate(plan):
        for k, d in enumerate(ds):
            for c in range(CORES):
                field = CORES * lax.rem(here + d, chips) + lax.rem(core + c, CORES)
                picked = (counts >> (FIELD * field)) & ((1 << FIELD) - 1)
                totals[number][0, k, c] += jnp.dot(
                    picked.astype(F32).astype(BF16), grads, preferred_element_type=F32
                )
    if first:
        return

    @pl.when(pl.program_id(1) == pl.num_programs(1) - 1)
    def _():
        at = 0
        for number, ds in enumerate(plan):
            for k in range(len(ds)):
                outs[at][...] = totals[number][0, k].astype(outs[at].dtype)
                at += 1


def row_sums(hst, counts, grads, befores, plan, table):
    tables, groups, words, columns = counts.shape
    group = grads.shape[0] // groups
    samples = columns // group
    begin = 0 if table is None else table
    count = tables if table is None else 1
    specs = [
        pl.BlockSpec((1, 1, words, columns), lambda t, g, hst: (begin + t, g, 0, 0)),
        pl.BlockSpec((group, samples, LANES), lambda t, g, hst: (g, 0, begin + t)),
    ]
    blocks = [
        pl.BlockSpec(
            (1, len(ds), CORES, words, LANES), lambda t, g, hst: (begin + t, 0, 0, 0, 0)
        )
        for ds in plan
    ]
    specs += blocks if befores else []
    scratch = []
    if table is None:
        out_specs = blocks
        out_shape = [
            jax.ShapeDtypeStruct((tables, len(ds), CORES, words, LANES), F32) for ds in plan
        ]
    else:
        every = [d for ds in plan for d in ds]
        out_specs = [
            pl.BlockSpec((CORES, words, LANES), lambda t, g, hst: (0, 0, 0)) for d in every
        ]
        out_shape = [
            jax.ShapeDtypeStruct((CORES, words, LANES), BF16 if d else F32) for d in every
        ]
        scratch = [pltpu.VMEM((1, len(ds), CORES, words, LANES), F32) for ds in plan]
    used = sum(len(ds) for ds in plan)
    return pl.pallas_call(
        functools.partial(sum_kernel, plan, not befores),
        grid_spec=pltpu.PrefetchScalarGridSpec(
            num_scalar_prefetch=1,
            grid=(count, groups),
            in_specs=specs,
            out_specs=out_specs,
            scratch_shapes=scratch,
        ),
        out_shape=out_shape,
        compiler_params=params(),
        cost_estimate=cost(count * groups * columns * used / 1600),
    )(hst, counts, grads, *befores)


def adagrad(number, grads, weights_ref, accum, new_weights_ref):
    rows, lanes = grads.shape
    mean = jnp.sum(grads * grads, 1, keepdims=True) * (1.0 / lanes)
    accum = jnp.broadcast_to(accum, (lanes, rows)).T + mean
    new_weights_ref[number] = weights_ref[number] - LEARN_RATE * grads / (
        jnp.sqrt(accum) + EPSILON
    )
    return accum.T[0:1]


def own_kernel(pieces, core_ref, weights_ref, accum_ref, *rest):
    piece_refs, (new_weights_ref, new_accum_ref, send_ref) = rest[:-3], rest[-3:]
    held = weights_ref.shape[0]
    mine = core_ref[0] == 0
    rows = []
    for t in range(held):
        total = piece_refs[t * pieces][...]
        for piece_ref in piece_refs[t * pieces + 1 : (t + 1) * pieces]:
            total = total + piece_ref[...].astype(F32)
        send_ref[t] = total[1].astype(BF16)
        accum = jnp.where(mine, accum_ref[t : t + 1], accum_ref[held + t : held + t + 1])
        rows.append(adagrad(t, total[0], weights_ref, accum, new_weights_ref))
    new_accum_ref[...] = jnp.concatenate(rows, 0)


def other_kernel(core_ref, weights_ref, accum_ref, grads_ref, own_accum_ref, *rest):
    new_weights_ref, new_accum_ref = rest[-2:]
    held = weights_ref.shape[0]
    mine = core_ref[0] == 0
    rows = []
    for t in range(held):
        accum = jnp.where(mine, accum_ref[held + t : held + t + 1], accum_ref[t : t + 1])
        grads = grads_ref[t].astype(F32)
        rows.append(adagrad(t, grads, weights_ref, accum, new_weights_ref))
    other, own = jnp.concatenate(rows, 0), own_accum_ref[...]
    new_accum_ref[...] = jnp.concatenate(
        [jnp.where(mine, own, other), jnp.where(mine, other, own)], 0
    )


def update(core, weights, accum, pieces):
    tables, words, lanes = weights.shape
    held = tables // CORES
    part = 256
    mine = pl.BlockSpec((held, part, lanes), lambda q, core: (core[0], q, 0))
    others = pl.BlockSpec((held, part, lanes), lambda q, core: (1 - core[0], q, 0))
    moved = pl.BlockSpec((held, part, lanes), lambda q, core: (0, q, 0))
    row = pl.BlockSpec((tables, part), lambda q, core: (0, q))
    half = pl.BlockSpec((held, part), lambda q, core: (0, q))
    piece = pl.BlockSpec((CORES, part, lanes), lambda q, core: (0, q, 0))
    flat = [array for table in pieces for array in table]
    new_weights, own_accum, send = pl.pallas_call(
        functools.partial(own_kernel, len(pieces[0])),
        grid_spec=pltpu.PrefetchScalarGridSpec(
            num_scalar_prefetch=1,
            grid=(words // part,),
            in_specs=[mine, row] + [piece] * len(flat),
            out_specs=[mine, half, moved],
        ),
        out_shape=[
            jax.ShapeDtypeStruct(weights.shape, F32),
            jax.ShapeDtypeStruct((held, words), F32),
            jax.ShapeDtypeStruct((held, words, lanes), BF16),
        ],
        compiler_params=params(SMALL),
        cost_estimate=cost(3),
    )(core, weights, accum, *flat)
    grads = lax.ppermute(send, "core", [(0, 1), (1, 0)])
    return pl.pallas_call(
        other_kernel,
        grid_spec=pltpu.PrefetchScalarGridSpec(
            num_scalar_prefetch=1,
            grid=(words // part,),
            in_specs=[others, row, moved, half, pl.BlockSpec(memory_space=pl.ANY)],
            out_specs=[others, row],
        ),
        out_shape=[
            jax.ShapeDtypeStruct(weights.shape, F32),
            jax.ShapeDtypeStruct(accum.shape, F32),
        ],
        input_output_aliases={5: 0},
        compiler_params=params(SMALL),
        cost_estimate=cost(2),
    )(core, weights, accum, grads, own_accum, new_weights)


def local(dense_out, pooled, dense_cot, pair_cot, bag_ids, weights, accum):
    samples = dense_out.shape[0]
    tables, slots, _ = bag_ids.shape
    words = weights.shape[1]
    chips = lax.axis_size("chip")
    devices = chips * CORES
    owners = lax.axis_size("wide") * CORES
    held = tables // owners
    core = lax.axis_index("core")
    hst = (lax.axis_index("chip") * CORES + core).reshape(1)

    def spread(x):
        return lax.all_to_all(x, ("wide", "core"), split_axis=0, concat_axis=0, tiled=True)

    args = (dense_out, pooled, dense_cot, pair_cot)
    late = samples - EARLY
    early_dense, send = interact(*args, bag_ids, owners, 0, EARLY)
    received = spread(send)
    late_dense, send = interact(*args, None, owners, EARLY, late)
    d_dense = jnp.concatenate([early_dense, late_dense], 0)
    early_counts = bag_counts(received, held, slots, words, 0, EARLY, 16)
    late_counts = bag_counts(received, held, slots, words, EARLY, late, LATE_GROUP)
    away, stay = tuple(range(1, chips)), (0,)
    leaving, staying = row_sums(hst, early_counts, received, (), (away, stay), None)
    received = spread(send)
    pieces = []
    for t in range(held):
        if t < held - 1:
            plan, befores = (away, stay), (leaving, staying)
        else:
            plan, befores = (away,), (leaving,)
        sums = row_sums(hst, late_counts, received, befores, plan, t)
        moved = []
        for d in away:
            ring = [(i, (i + d) % chips) for i in range(chips)]
            moved.append(lax.ppermute(sums[d - 1], "chip", ring))
        pieces.append([sums[-1]] + moved)
    pieces[-1][0] = row_sums(hst, late_counts, received, (staying,), (stay,), held - 1)[0]
    new_weights, new_accum = update(core.reshape(1), weights, accum, pieces)
    return d_dense, new_weights, new_accum


def solution(mesh):
    hst, wide = mesh.devices.shape
    split = Mesh(mesh.devices.reshape(hst // CORES, CORES, wide), ("chip", "core", "wide"))
    every = ("chip", "core", "wide")
    rows = ("chip", "core")
    in_specs = (
        P(every, None),
        P(every, None),
        P(every, None),
        P(every, None),
        P(None, None, every),
        P("wide", rows, None),
        P("wide", rows),
    )
    out_specs = (P(every, None), P("wide", rows, None), P("wide", rows))
    return jax.shard_map(local, mesh=split, in_specs=in_specs, out_specs=out_specs, check_vma=False)
```

```python
import functools

import jax
import jax.numpy as jnp
from jax import lax
from jax.experimental import pallas as pl
from jax.experimental.pallas import tpu as pltpu
from jax.sharding import Mesh
from jax.sharding import PartitionSpec as P

LEARN_RATE = 0.5
EPSILON = 1e-08
LANES = 128
HALF = 64
FIELD = 4
BLOCK = 32
CORES = 2
CODE = 7
STRIP = 64
VMEM = 40 << 20
FULL = 62 << 20
SMALL = 12 << 20
EARLY = 64
GROUP = 8
AWAY = (1, 2, 3)
BF16 = jnp.bfloat16
F32 = jnp.float32


def cost(micros):
    return pl.CostEstimate(flops=int(micros * 2e8), bytes_accessed=1 << 16, transcendentals=0)


def in_hbm(x):
    return pltpu.with_memory_space_constraint(x, pltpu.HBM)


def params(size=VMEM):
    return pltpu.CompilerParams(vmem_limit_bytes=size)


def encode(ids):
    high = lax.shift_right_logical(ids, CODE)
    value = ((1 << CODE) + (ids & ((1 << CODE) - 1))).astype(F32)
    for bit in range(5):
        value = jnp.where((high >> bit) & 1 == 1, value * 2.0 ** (1 << bit), value)
    return value.astype(BF16)


def decode(codes):
    value = codes.astype(F32)
    high = jnp.zeros(value.shape, jnp.int32)
    for bit in range(4, -1, -1):
        large = value >= 2.0 ** (CODE + (1 << bit))
        value = jnp.where(large, value * 2.0 ** -(1 << bit), value)
        high = jnp.where(large, high + (1 << bit), high)
    return (high << CODE) + value.astype(jnp.int32) - (1 << CODE)


def interact_kernel(steps, with_ids, dense_ref, pooled_ref, cot_ref, pair_ref, *rest):
    if with_ids:
        ids_ref, *rest = rest
    d_dense_ref, send_ref, *scratch = rest
    tables = pooled_ref.shape[1] // LANES
    held = tables // send_ref.shape[0]

    @pl.when(pl.program_id(0) == 0)
    def _():
        for ref in scratch[1:3]:
            ref[...] = jnp.zeros_like(ref)

    if not with_ids:
        interact_block(dense_ref, pooled_ref, cot_ref, pair_ref, d_dense_ref, send_ref, *scratch)
        return

    @pl.when(pl.program_id(0) < steps)
    def _():
        interact_block(dense_ref, pooled_ref, cot_ref, pair_ref, d_dense_ref, send_ref, *scratch)

    @pl.when(pl.program_id(0) == steps)
    def _():
        slots = ids_ref.shape[1]
        for owner in range(tables // held):
            ids = ids_ref[owner * held : (owner + 1) * held]
            send_ref[owner, 0 : held * slots, :] = encode(ids.reshape(held * slots, -1))


def interact_block(
    dense_ref, pooled_ref, cot_ref, pair_ref, d_dense_ref, send_ref, wide_pairs, lower, feats, grads
):
    block = dense_ref.shape[0]
    half = block // 2
    tables = pooled_ref.shape[1] // LANES
    rows = lower.shape[1]

    wide_pairs[:, 0 : pair_ref.shape[1]] = pair_ref[...].astype(F32)
    lane = lax.broadcasted_iota(jnp.int32, (half, LANES), 1)
    for i in range(1, tables + 1):
        start = i * (i - 1) // 2
        base = start // LANES * LANES
        shift = start - base
        to_low = (LANES - shift) % LANES
        to_high = (HALF - shift) % LANES

        def rolled(first, amount, at):
            piece = wide_pairs[first : first + half, at : at + LANES]
            return pltpu.roll(piece, amount, 1) if amount else piece

        low = rolled(0, to_low, base)
        high = rolled(half, to_high, base)
        if shift + i > LANES:
            low = jnp.where(lane < LANES - shift, low, rolled(0, to_low, base + LANES))
            high = jnp.where(
                lane < HALF + LANES - shift, high, rolled(half, to_high, base + LANES)
            )
        if i < HALF:
            low = jnp.where(lane < i, low, 0.0)
            high = jnp.where(lane < HALF + i, high, 0.0)
        lower[:, i, :] = jnp.where(lane < HALF, low, high)

    feats[:, 0, :] = dense_ref[...].astype(F32)
    for t in range(tables):
        feats[:, t + 1, :] = pooled_ref[:, t * LANES : (t + 1) * LANES].astype(F32)

    row_lane = lax.broadcasted_iota(jnp.int32, (rows, LANES), 1)
    below = jnp.zeros((rows - HALF, LANES), F32)

    def two_samples(b, carry):
        both = lower[b]
        turned = both.astype(BF16).T.astype(F32)
        turned = jnp.concatenate([turned, jnp.zeros((LANES, LANES - rows), F32)], 1)
        first = jnp.where(row_lane < HALF, both, 0.0)
        second = jnp.where(row_lane < HALF, pltpu.roll(both, HALF, 1), 0.0)
        first = first + jnp.concatenate([turned[:HALF], below], 0)
        second = second + jnp.concatenate([turned[HALF:], below], 0)
        for pairs, sample in ((first, b), (second, b + half)):
            out = jnp.dot(
                pairs[:, :rows].astype(BF16),
                feats[sample].astype(BF16),
                preferred_element_type=F32,
            )
            grads[:, pl.ds(sample, 1), :] = out.reshape(rows, 1, LANES)
        return carry

    lax.fori_loop(0, half, two_samples, 0, unroll=8)

    d_dense_ref[...] = (grads[0, 0:block] + cot_ref[...].astype(F32)).astype(BF16)
    owners = send_ref.shape[0]
    held = tables // owners
    for t in range(tables):
        place = t % held * LANES
        send_ref[t // held, :, place : place + LANES] = grads[t + 1, 0:block].astype(BF16)


def interact(dense_out, pooled, dense_cot, pair_cot, ids, owners, first):
    tables = pooled.shape[1] // LANES
    samples, pairs = pair_cot.shape
    held = tables // owners
    rows = (tables + 1 + 7) // 8 * 8
    padded = (pairs // LANES + 1) * LANES
    skip, steps = first // BLOCK, samples // BLOCK
    with_ids = ids is not None
    slots = ids.shape[1] if with_ids else 0

    def at(s):
        return (skip + jnp.minimum(s, steps - 1), 0)

    specs = [
        pl.BlockSpec((BLOCK, LANES), at),
        pl.BlockSpec((BLOCK, tables * LANES), at),
        pl.BlockSpec((BLOCK, LANES), at),
        pl.BlockSpec((BLOCK, pairs), lambda s: (jnp.minimum(s, steps - 1), 0)),
    ]
    operands = [in_hbm(x) for x in (dense_out, pooled, dense_cot, pair_cot)]
    if with_ids:
        specs.append(pl.BlockSpec(ids.shape, lambda s: (0, 0, 0)))
        operands.append(in_hbm(ids))
    extra = 1 if with_ids else 0
    return pl.pallas_call(
        functools.partial(interact_kernel, steps, with_ids),
        grid=(steps + extra,),
        in_specs=specs,
        out_specs=[
            pl.BlockSpec((BLOCK, LANES), lambda s: (jnp.minimum(s, steps - 1), 0)),
            pl.BlockSpec((owners, BLOCK, held * LANES), lambda s: (0, s, 0)),
        ],
        out_shape=[
            jax.ShapeDtypeStruct((samples, LANES), BF16),
            pltpu.HBM((owners, samples + extra * held * slots, held * LANES), BF16),
        ],
        scratch_shapes=[
            pltpu.VMEM((BLOCK, padded), F32),
            pltpu.VMEM((BLOCK // 2, rows, LANES), F32),
            pltpu.VMEM((BLOCK, rows, LANES), F32),
            pltpu.VMEM((rows, BLOCK + 8, LANES), F32),
        ],
        compiler_params=params(FULL),
        cost_estimate=cost(20 * samples / 256),
    )(*operands)


def slot_words(first, samples, words, table, codes_ref):
    sources, rows, _ = codes_ref.shape
    slots = 32 // FIELD
    bits = words.bit_length() - 1
    codes = jnp.concatenate(
        [codes_ref[source, :, first : first + samples] for source in range(sources)], 1
    ).astype(F32)
    mine = codes[:slots]
    for other in range(1, rows // slots):
        mine = jnp.where(table == other, codes[other * slots : (other + 1) * slots], mine)
    ids = decode(mine)
    word = ids & (words - 1)
    one = jnp.left_shift(1, FIELD * lax.shift_right_logical(ids, bits))
    total = one
    for by in range(1, slots):
        total = total + jnp.where(word == pltpu.roll(word, by, 0), pltpu.roll(one, by, 0), 0)
    return word, total


def count_column(word, total, at, out_ref):
    words = out_ref.shape[0]
    slots = word.shape[0]
    place = lax.broadcasted_iota(jnp.int32, (STRIP, LANES), 0)
    words_at = [word[slot : slot + 1, at : at + LANES] for slot in range(slots)]
    totals_at = [total[slot : slot + 1, at : at + LANES] for slot in range(slots)]
    for start in range(0, words, STRIP):
        out = jnp.zeros((STRIP, LANES), jnp.int32)
        for slot in range(slots):
            out = jnp.where(words_at[slot] == place + start, totals_at[slot], out)
        out_ref[start : start + STRIP, at : at + LANES] = out


def early_kernel(late, hst_ref, grads_ref, codes_ref, total_ref, late_ref, counts_ref):
    @pl.when(pl.program_id(1) == 0)
    def _():
        total_ref[...] = jnp.zeros_like(total_ref)

    group, samples, _ = grads_ref.shape
    chips = total_ref.shape[1]
    fields = chips * CORES
    words = counts_ref.shape[0]
    table = pl.program_id(0)
    word, total = slot_words(0, samples, words, table, codes_ref)
    for at in range(0, counts_ref.shape[1], LANES):
        count_column(word, total, at, counts_ref)
    grads = grads_ref[...].reshape(group * samples, LANES)
    word, total = slot_words(samples, late, words, table, codes_ref)
    lanes = list(range(0, late_ref.shape[3], LANES))
    here, core = hst_ref[0] // CORES, lax.rem(hst_ref[0], CORES)
    for field in range(fields):
        if field < fields - 1:
            taken, scale = counts_ref[...] & (((1 << FIELD) - 1) << (FIELD * field)), FIELD * field
        else:
            taken, scale = lax.shift_right_logical(counts_ref[...], FIELD * field), 0
        part = jnp.dot(
            taken.astype(F32).astype(BF16), grads, preferred_element_type=F32
        )
        chip = lax.rem(field // CORES + 2 * chips - 1 - here, chips)
        c = lax.rem(field + core, CORES)
        total_ref[0, chip, c] += part * 2.0**-scale
        begin, end = (len(lanes) * n // fields for n in (field, field + 1))
        for at in lanes[begin:end]:
            count_column(word, total, at, late_ref.at[0, 0])


def early_sums(hst, received, held, slots, words, early, late, chips):
    sources, rows, lanes = received.shape
    groups = sources // GROUP
    codes = held * slots
    last = rows // codes - 1
    totals = (chips, CORES, words, LANES)
    return pl.pallas_call(
        functools.partial(early_kernel, late),
        grid_spec=pltpu.PrefetchScalarGridSpec(
            num_scalar_prefetch=1,
            grid=(held, groups),
            in_specs=[
                pl.BlockSpec((GROUP, early, LANES), lambda t, g, hst: (g, 0, t)),
                pl.BlockSpec((GROUP, codes, lanes), lambda t, g, hst: (g, last, 0)),
            ],
            out_specs=[
                pl.BlockSpec((1,) + totals, lambda t, g, hst: (t, 0, 0, 0, 0)),
                pl.BlockSpec((1, 1, words, GROUP * late), lambda t, g, hst: (t, g, 0, 0)),
            ],
            scratch_shapes=[pltpu.VMEM((words, GROUP * early), jnp.int32)],
        ),
        out_shape=[
            jax.ShapeDtypeStruct((held,) + totals, F32),
            pltpu.HBM((held, groups, words, GROUP * late), jnp.int32),
        ],
        compiler_params=params(FULL),
        cost_estimate=cost(25),
    )(hst, in_hbm(received), in_hbm(received))


def picked(counts, hst_ref, d, c):
    chips = 32 // FIELD // CORES
    here, core = hst_ref[0] // CORES, lax.rem(hst_ref[0], CORES)
    field = CORES * lax.rem(here + d, chips) + lax.rem(core + c, CORES)
    return ((counts >> (FIELD * field)) & ((1 << FIELD) - 1)).astype(F32).astype(BF16)


def sum_kernel(ds, hst_ref, counts_ref, grads_ref, before_ref, *rest):
    outs, total = rest[:-1], rest[-1]

    @pl.when(pl.program_id(0) == 0)
    def _():
        total[...] = before_ref[0]

    group, samples, _ = grads_ref.shape
    grads = grads_ref[...].reshape(group * samples, LANES)
    counts = counts_ref[0, 0]
    for k, d in enumerate(ds):
        for c in range(CORES):
            total[k, c] += jnp.dot(
                picked(counts, hst_ref, d, c), grads, preferred_element_type=F32
            )

    @pl.when(pl.program_id(0) == pl.num_programs(0) - 1)
    def _():
        for k, out in enumerate(outs):
            out[...] = total[k].astype(out.dtype)


def row_sums(hst, counts, grads, before, ds, table):
    _, groups, words, columns = counts.shape
    group = grads.shape[0] // groups
    samples = columns // group
    at = (ds[0] - 1) % before.shape[1] // len(ds)
    return pl.pallas_call(
        functools.partial(sum_kernel, ds),
        grid_spec=pltpu.PrefetchScalarGridSpec(
            num_scalar_prefetch=1,
            grid=(groups,),
            in_specs=[
                pl.BlockSpec((1, 1, words, columns), lambda g, hst: (table, g, 0, 0)),
                pl.BlockSpec((group, samples, LANES), lambda g, hst: (g, 0, table)),
                pl.BlockSpec(
                    (1, len(ds), CORES, words, LANES), lambda g, hst: (table, at, 0, 0, 0)
                ),
            ],
            out_specs=[
                pl.BlockSpec((CORES, words, LANES), lambda g, hst: (0, 0, 0)) for d in ds
            ],
            scratch_shapes=[pltpu.VMEM((len(ds), CORES, words, LANES), F32)],
        ),
        out_shape=[
            jax.ShapeDtypeStruct((CORES, words, LANES), BF16 if d else F32) for d in ds
        ],
        compiler_params=params(),
        cost_estimate=cost(2 * len(ds)),
    )(hst, in_hbm(counts), in_hbm(grads), before)


def adagrad(number, grads, weights_ref, accum, new_weights_ref):
    rows, lanes = grads.shape
    mean = jnp.sum(grads * grads, 1, keepdims=True) * (1.0 / lanes)
    accum = jnp.broadcast_to(accum, (lanes, rows)).T + mean
    new_weights_ref[number] = weights_ref[number] - LEARN_RATE * grads / (
        jnp.sqrt(accum) + EPSILON
    )
    return accum.T[0:1]


def own_kernel(pieces, core_ref, weights_ref, accum_ref, *rest):
    piece_refs, (new_weights_ref, new_accum_ref, send_ref) = rest[:-3], rest[-3:]
    held = weights_ref.shape[0]
    mine = core_ref[0] == 0
    rows = []
    for t in range(held):
        total = piece_refs[t * pieces][...]
        for piece_ref in piece_refs[t * pieces + 1 : (t + 1) * pieces]:
            total = total + piece_ref[...].astype(F32)
        send_ref[t] = total[1].astype(BF16)
        accum = jnp.where(mine, accum_ref[t : t + 1], accum_ref[held + t : held + t + 1])
        rows.append(adagrad(t, total[0], weights_ref, accum, new_weights_ref))
    new_accum_ref[...] = jnp.concatenate(rows, 0)


def other_kernel(core_ref, weights_ref, accum_ref, grads_ref, own_accum_ref, *rest):
    new_weights_ref, new_accum_ref = rest[-2:]
    held = weights_ref.shape[0]
    mine = core_ref[0] == 0
    rows = []
    for t in range(held):
        accum = jnp.where(mine, accum_ref[held + t : held + t + 1], accum_ref[t : t + 1])
        grads = grads_ref[t].astype(F32)
        rows.append(adagrad(t, grads, weights_ref, accum, new_weights_ref))
    other, own = jnp.concatenate(rows, 0), own_accum_ref[...]
    new_accum_ref[...] = jnp.concatenate(
        [jnp.where(mine, own, other), jnp.where(mine, other, own)], 0
    )


def update(core, weights, accum, pieces):
    tables, words, lanes = weights.shape
    held = tables // CORES
    part = 256
    mine = pl.BlockSpec((held, part, lanes), lambda q, core: (core[0], q, 0))
    others = pl.BlockSpec((held, part, lanes), lambda q, core: (1 - core[0], q, 0))
    moved = pl.BlockSpec((held, part, lanes), lambda q, core: (0, q, 0))
    row = pl.BlockSpec((tables, part), lambda q, core: (0, q))
    half = pl.BlockSpec((held, part), lambda q, core: (0, q))
    piece = pl.BlockSpec((CORES, part, lanes), lambda q, core: (0, q, 0))
    flat = [array for table in pieces for array in table]
    new_weights, own_accum, send = pl.pallas_call(
        functools.partial(own_kernel, len(pieces[0])),
        grid_spec=pltpu.PrefetchScalarGridSpec(
            num_scalar_prefetch=1,
            grid=(words // part,),
            in_specs=[mine, row] + [piece] * len(flat),
            out_specs=[mine, half, moved],
        ),
        out_shape=[
            jax.ShapeDtypeStruct(weights.shape, F32),
            jax.ShapeDtypeStruct((held, words), F32),
            jax.ShapeDtypeStruct((held, words, lanes), BF16),
        ],
        compiler_params=params(SMALL),
        cost_estimate=cost(3),
    )(core, weights, accum, *flat)
    grads = lax.ppermute(send, "core", [(0, 1), (1, 0)])
    return pl.pallas_call(
        other_kernel,
        grid_spec=pltpu.PrefetchScalarGridSpec(
            num_scalar_prefetch=1,
            grid=(words // part,),
            in_specs=[others, row, moved, half, pl.BlockSpec(memory_space=pl.ANY)],
            out_specs=[others, row],
        ),
        out_shape=[
            jax.ShapeDtypeStruct(weights.shape, F32),
            jax.ShapeDtypeStruct(accum.shape, F32),
        ],
        input_output_aliases={5: 0},
        compiler_params=params(SMALL),
        cost_estimate=cost(2),
    )(core, weights, accum, grads, own_accum, new_weights)


def local(dense_out, pooled, dense_cot, pair_cot, bag_ids, weights, accum):
    samples = dense_out.shape[0]
    tables, slots, _ = bag_ids.shape
    words = weights.shape[1]
    chips = lax.axis_size("chip")
    devices = chips * CORES
    owners = lax.axis_size("wide") * CORES
    held = tables // owners
    core = lax.axis_index("core")
    hst = (lax.axis_index("chip") * CORES + core).reshape(1)

    def spread(x):
        return lax.all_to_all(x, ("wide", "core"), split_axis=0, concat_axis=0, tiled=True)

    late = samples - EARLY
    early_pairs, late_pairs = pair_cot[:EARLY], pair_cot[EARLY:]
    early_dense, send = interact(dense_out, pooled, dense_cot, early_pairs, bag_ids, owners, 0)
    received = spread(send)
    late_dense, send = interact(dense_out, pooled, dense_cot, late_pairs, None, owners, EARLY)
    d_dense = jnp.concatenate([early_dense, late_dense], 0)
    before, counts = early_sums(hst, received, held, slots, words, EARLY, late, chips)
    received = spread(send)
    pieces = []
    for t in range(held):
        everything = t < held - 1
        prior = before if t else in_hbm(before)
        sums = list(row_sums(hst, counts, received, prior, AWAY + (0,) * everything, t))
        before, sums[0] = lax.optimization_barrier((before, sums[0]))
        moved = []
        for d in AWAY:
            ring = [(i, (i + d) % chips) for i in range(chips)]
            moved.append(lax.ppermute(sums[d - 1], "chip", ring))
        pieces.append(sums[len(AWAY) :] + moved)
    pieces[-1] = list(row_sums(hst, counts, received, before, (0,), held - 1)) + pieces[-1]
    new_weights, new_accum = update(core.reshape(1), weights, accum, pieces)
    return d_dense, new_weights, new_accum


def solution(mesh):
    hst, wide = mesh.devices.shape
    split = Mesh(mesh.devices.reshape(hst // CORES, CORES, wide), ("chip", "core", "wide"))
    every = ("chip", "core", "wide")
    rows = ("chip", "core")
    in_specs = (
        P(every, None),
        P(every, None),
        P(every, None),
        P(every, None),
        P(None, None, every),
        P("wide", rows, None),
        P("wide", rows),
    )
    out_specs = (P(every, None), P("wide", rows, None), P("wide", rows))
    return jax.shard_map(local, mesh=split, in_specs=in_specs, out_specs=out_specs, check_vma=False)
```

```python
import functools

import jax
import jax.numpy as jnp
from jax import lax
from jax.experimental import pallas as pl
from jax.experimental.pallas import tpu as pltpu
from jax.sharding import Mesh
from jax.sharding import PartitionSpec as P

LEARN_RATE = 0.5
EPSILON = 1e-08
LANES = 128
HALF = 64
FIELD = 4
BLOCK = 32
CORES = 2
CODE = 7
STRIP = 64
VMEM = 40 << 20
FULL = 62 << 20
SMALL = 12 << 20
EARLY = 64
GROUP = 8
AWAY = (1, 2, 3)
BF16 = jnp.bfloat16
F32 = jnp.float32


def cost(micros):
    return pl.CostEstimate(flops=int(micros * 2e8), bytes_accessed=1 << 16, transcendentals=0)


def in_hbm(x):
    return pltpu.with_memory_space_constraint(x, pltpu.HBM)


def params(size=VMEM):
    return pltpu.CompilerParams(vmem_limit_bytes=size)


def encode(ids):
    high = lax.shift_right_logical(ids, CODE)
    value = ((1 << CODE) + (ids & ((1 << CODE) - 1))).astype(F32)
    for bit in range(5):
        value = jnp.where((high >> bit) & 1 == 1, value * 2.0 ** (1 << bit), value)
    return value.astype(BF16)


def decode(codes):
    value = codes.astype(F32)
    high = jnp.zeros(value.shape, jnp.int32)
    for bit in range(4, -1, -1):
        large = value >= 2.0 ** (CODE + (1 << bit))
        value = jnp.where(large, value * 2.0 ** -(1 << bit), value)
        high = jnp.where(large, high + (1 << bit), high)
    return (high << CODE) + value.astype(jnp.int32) - (1 << CODE)


def interact_kernel(steps, with_ids, dense_ref, pooled_ref, cot_ref, pair_ref, *rest):
    if with_ids:
        ids_ref, *rest = rest
    d_dense_ref, send_ref, *scratch = rest
    tables = pooled_ref.shape[1] // LANES
    held = tables // send_ref.shape[0]

    @pl.when(pl.program_id(0) == 0)
    def _():
        for ref in scratch[1:3]:
            ref[...] = jnp.zeros_like(ref)

    if not with_ids:
        interact_block(dense_ref, pooled_ref, cot_ref, pair_ref, d_dense_ref, send_ref, *scratch)
        return

    @pl.when(pl.program_id(0) < steps)
    def _():
        interact_block(dense_ref, pooled_ref, cot_ref, pair_ref, d_dense_ref, send_ref, *scratch)

    @pl.when(pl.program_id(0) == steps)
    def _():
        slots = ids_ref.shape[1]
        for owner in range(tables // held):
            ids = ids_ref[owner * held : (owner + 1) * held]
            send_ref[owner, 0 : held * slots, :] = encode(ids.reshape(held * slots, -1))


def interact_block(
    dense_ref, pooled_ref, cot_ref, pair_ref, d_dense_ref, send_ref, wide_pairs, lower, feats, grads
):
    block = dense_ref.shape[0]
    half = block // 2
    tables = pooled_ref.shape[1] // LANES
    rows = lower.shape[1]

    wide_pairs[:, 0 : pair_ref.shape[1]] = pair_ref[...].astype(F32)
    lane = lax.broadcasted_iota(jnp.int32, (half, LANES), 1)
    for i in range(1, tables + 1):
        start = i * (i - 1) // 2
        base = start // LANES * LANES
        shift = start - base
        to_low = (LANES - shift) % LANES
        to_high = (HALF - shift) % LANES

        def rolled(first, amount, at):
            piece = wide_pairs[first : first + half, at : at + LANES]
            return pltpu.roll(piece, amount, 1) if amount else piece

        low = rolled(0, to_low, base)
        high = rolled(half, to_high, base)
        if shift + i > LANES:
            low = jnp.where(lane < LANES - shift, low, rolled(0, to_low, base + LANES))
            high = jnp.where(
                lane < HALF + LANES - shift, high, rolled(half, to_high, base + LANES)
            )
        if i < HALF:
            low = jnp.where(lane < i, low, 0.0)
            high = jnp.where(lane < HALF + i, high, 0.0)
        lower[:, i, :] = jnp.where(lane < HALF, low, high)

    feats[:, 0, :] = dense_ref[...].astype(F32)
    for t in range(tables):
        feats[:, t + 1, :] = pooled_ref[:, t * LANES : (t + 1) * LANES].astype(F32)

    row_lane = lax.broadcasted_iota(jnp.int32, (rows, LANES), 1)
    below = jnp.zeros((rows - HALF, LANES), F32)

    def two_samples(b, carry):
        both = lower[b]
        turned = both.astype(BF16).T.astype(F32)
        turned = jnp.concatenate([turned, jnp.zeros((LANES, LANES - rows), F32)], 1)
        first = jnp.where(row_lane < HALF, both, 0.0)
        second = jnp.where(row_lane < HALF, pltpu.roll(both, HALF, 1), 0.0)
        first = first + jnp.concatenate([turned[:HALF], below], 0)
        second = second + jnp.concatenate([turned[HALF:], below], 0)
        for pairs, sample in ((first, b), (second, b + half)):
            out = jnp.dot(
                pairs[:, :rows].astype(BF16),
                feats[sample].astype(BF16),
                preferred_element_type=F32,
            )
            grads[:, pl.ds(sample, 1), :] = out.reshape(rows, 1, LANES)
        return carry

    lax.fori_loop(0, half, two_samples, 0, unroll=8)

    d_dense_ref[...] = (grads[0, 0:block] + cot_ref[...].astype(F32)).astype(BF16)
    owners = send_ref.shape[0]
    held = tables // owners
    for t in range(tables):
        place = t % held * LANES
        send_ref[t // held, :, place : place + LANES] = grads[t + 1, 0:block].astype(BF16)


def interact(dense_out, pooled, dense_cot, pair_cot, ids, owners, first):
    tables = pooled.shape[1] // LANES
    samples, pairs = pair_cot.shape
    held = tables // owners
    rows = (tables + 1 + 7) // 8 * 8
    padded = (pairs // LANES + 1) * LANES
    skip, steps = first // BLOCK, samples // BLOCK
    with_ids = ids is not None
    slots = ids.shape[1] if with_ids else 0

    def at(s):
        return (skip + jnp.minimum(s, steps - 1), 0)

    specs = [
        pl.BlockSpec((BLOCK, LANES), at),
        pl.BlockSpec((BLOCK, tables * LANES), at),
        pl.BlockSpec((BLOCK, LANES), at),
        pl.BlockSpec((BLOCK, pairs), lambda s: (jnp.minimum(s, steps - 1), 0)),
    ]
    operands = [in_hbm(x) for x in (dense_out, pooled, dense_cot, pair_cot)]
    if with_ids:
        specs.append(pl.BlockSpec(ids.shape, lambda s: (0, 0, 0)))
        operands.append(in_hbm(ids))
    extra = 1 if with_ids else 0
    return pl.pallas_call(
        functools.partial(interact_kernel, steps, with_ids),
        grid=(steps + extra,),
        in_specs=specs,
        out_specs=[
            pl.BlockSpec((BLOCK, LANES), lambda s: (jnp.minimum(s, steps - 1), 0)),
            pl.BlockSpec((owners, BLOCK, held * LANES), lambda s: (0, s, 0)),
        ],
        out_shape=[
            jax.ShapeDtypeStruct((samples, LANES), BF16),
            pltpu.HBM((owners, samples + extra * held * slots, held * LANES), BF16),
        ],
        scratch_shapes=[
            pltpu.VMEM((BLOCK, padded), F32),
            pltpu.VMEM((BLOCK // 2, rows, LANES), F32),
            pltpu.VMEM((BLOCK, rows, LANES), F32),
            pltpu.VMEM((rows, BLOCK + 8, LANES), F32),
        ],
        compiler_params=params(FULL),
        cost_estimate=cost(20 * samples / 256),
    )(*operands)


def slot_words(first, samples, words, table, codes_ref):
    sources, rows, _ = codes_ref.shape
    slots = 32 // FIELD
    bits = words.bit_length() - 1
    codes = jnp.concatenate(
        [codes_ref[source, :, first : first + samples] for source in range(sources)], 1
    ).astype(F32)
    mine = codes[:slots]
    for other in range(1, rows // slots):
        mine = jnp.where(table == other, codes[other * slots : (other + 1) * slots], mine)
    ids = decode(mine)
    word = ids & (words - 1)
    one = jnp.left_shift(1, FIELD * lax.shift_right_logical(ids, bits))
    total = one
    for by in range(1, slots):
        total = total + jnp.where(word == pltpu.roll(word, by, 0), pltpu.roll(one, by, 0), 0)
    return word, total


def count_column(word, total, at, out_ref):
    words = out_ref.shape[0]
    slots = word.shape[0]
    place = lax.broadcasted_iota(jnp.int32, (STRIP, LANES), 0)
    words_at = [word[slot : slot + 1, at : at + LANES] for slot in range(slots)]
    totals_at = [total[slot : slot + 1, at : at + LANES] for slot in range(slots)]
    for start in range(0, words, STRIP):
        out = jnp.zeros((STRIP, LANES), jnp.int32)
        for slot in range(slots):
            out = jnp.where(words_at[slot] == place + start, totals_at[slot], out)
        out_ref[start : start + STRIP, at : at + LANES] = out


def early_kernel(late, hst_ref, grads_ref, codes_ref, total_ref, late_ref, own_ref, counts_ref):
    @pl.when(pl.program_id(1) == 0)
    def _():
        total_ref[...] = jnp.zeros_like(total_ref)

    group, samples, _ = grads_ref.shape
    chips = total_ref.shape[1]
    fields = chips * CORES
    words = counts_ref.shape[0]
    table = pl.program_id(0)
    word, total = slot_words(0, samples, words, table, codes_ref)
    for at in range(0, counts_ref.shape[1], LANES):
        count_column(word, total, at, counts_ref)
    grads = grads_ref[...].reshape(group * samples, LANES)
    word, total = slot_words(samples, late, words, table, codes_ref)
    lanes = list(range(0, late_ref.shape[3], LANES))
    here, core = hst_ref[0] // CORES, lax.rem(hst_ref[0], CORES)
    for field in range(fields):
        if field < fields - 1:
            taken, scale = counts_ref[...] & (((1 << FIELD) - 1) << (FIELD * field)), FIELD * field
        else:
            taken, scale = lax.shift_right_logical(counts_ref[...], FIELD * field), 0
        part = jnp.dot(
            taken.astype(F32).astype(BF16), grads, preferred_element_type=F32
        )
        chip = lax.rem(field // CORES + 2 * chips - 1 - here, chips)
        c = lax.rem(field + core, CORES)
        total_ref[0, chip, c] += part * 2.0**-scale
        begin, end = (len(lanes) * n // fields for n in (field, field + 1))
        for at in lanes[begin:end]:
            count_column(word, total, at, late_ref.at[0, 0])
            columns = slice(at, at + LANES)
            for c in range(CORES):
                field = CORES * here + lax.rem(core + c, CORES)
                own = (late_ref[0, 0, :, columns] >> (FIELD * field)) & ((1 << FIELD) - 1)
                own_ref[0, 0, c, :, columns] = own.astype(jnp.int8)


def early_sums(hst, received, held, slots, words, early, late, chips):
    sources, rows, lanes = received.shape
    groups = sources // GROUP
    codes = held * slots
    last = rows // codes - 1
    totals = (chips, CORES, words, LANES)
    return pl.pallas_call(
        functools.partial(early_kernel, late),
        grid_spec=pltpu.PrefetchScalarGridSpec(
            num_scalar_prefetch=1,
            grid=(held, groups),
            in_specs=[
                pl.BlockSpec((GROUP, early, LANES), lambda t, g, hst: (g, 0, t)),
                pl.BlockSpec((GROUP, codes, lanes), lambda t, g, hst: (g, last, 0)),
            ],
            out_specs=[
                pl.BlockSpec((1,) + totals, lambda t, g, hst: (t, 0, 0, 0, 0)),
                pl.BlockSpec((1, 1, words, GROUP * late), lambda t, g, hst: (t, g, 0, 0)),
                pl.BlockSpec((1, 1, CORES, words, GROUP * late), lambda t, g, hst: (t, g, 0, 0, 0)),
            ],
            scratch_shapes=[pltpu.VMEM((words, GROUP * early), jnp.int32)],
        ),
        out_shape=[
            jax.ShapeDtypeStruct((held,) + totals, F32),
            pltpu.HBM((held, groups, words, GROUP * late), jnp.int32),
            pltpu.HBM((held, groups, CORES, words, GROUP * late), jnp.int8),
        ],
        compiler_params=params(FULL),
        cost_estimate=cost(25),
    )(hst, in_hbm(received), in_hbm(received))


def picked(counts, hst_ref, d, c):
    chips = 32 // FIELD // CORES
    here, core = hst_ref[0] // CORES, lax.rem(hst_ref[0], CORES)
    field = CORES * lax.rem(here + d, chips) + lax.rem(core + c, CORES)
    return ((counts >> (FIELD * field)) & ((1 << FIELD) - 1)).astype(F32).astype(BF16)


def sum_kernel(ds, hst_ref, counts_ref, grads_ref, before_ref, *rest):
    outs, total = rest[:-1], rest[-1]

    @pl.when(pl.program_id(1) == 0)
    def _():
        total[...] = before_ref[0]

    group, samples, _ = grads_ref.shape
    grads = grads_ref[...].reshape(group * samples, LANES)
    for k, d in enumerate(ds):
        for c in range(CORES):
            if d:
                counts = picked(counts_ref[0, 0], hst_ref, d, c)
            else:
                counts = counts_ref[0, 0, c].astype(BF16)
            total[k, c] += jnp.dot(counts, grads, preferred_element_type=F32)

    @pl.when(pl.program_id(1) == pl.num_programs(1) - 1)
    def _():
        for k, out in enumerate(outs):
            out[0] = total[k].astype(out.dtype)


def row_sums(hst, counts, grads, before, ds, first, tables):
    groups, words, columns = counts.shape[1], counts.shape[-2], counts.shape[-1]
    group = grads.shape[0] // groups
    samples = columns // group
    at = (ds[0] - 1) % before.shape[1] // len(ds)
    fixed = (0,) * (counts.ndim - 2)
    return pl.pallas_call(
        functools.partial(sum_kernel, ds),
        grid_spec=pltpu.PrefetchScalarGridSpec(
            num_scalar_prefetch=1,
            grid=(tables, groups),
            in_specs=[
                pl.BlockSpec((1, 1) + counts.shape[2:], lambda t, g, hst: (first + t, g) + fixed),
                pl.BlockSpec((group, samples, LANES), lambda t, g, hst: (g, 0, first + t)),
                pl.BlockSpec(
                    (1, len(ds), CORES, words, LANES), lambda t, g, hst: (first + t, at, 0, 0, 0)
                ),
            ],
            out_specs=[
                pl.BlockSpec((1, CORES, words, LANES), lambda t, g, hst: (t, 0, 0, 0)) for d in ds
            ],
            scratch_shapes=[pltpu.VMEM((len(ds), CORES, words, LANES), F32)],
        ),
        out_shape=[
            jax.ShapeDtypeStruct((tables, CORES, words, LANES), BF16 if d else F32) for d in ds
        ],
        compiler_params=params(),
        cost_estimate=cost(0.1),
    )(hst, in_hbm(counts), in_hbm(grads), before)


def adagrad(number, grads, weights_ref, accum, new_weights_ref):
    rows, lanes = grads.shape
    mean = jnp.sum(grads * grads, 1, keepdims=True) * (1.0 / lanes)
    accum = jnp.broadcast_to(accum, (lanes, rows)).T + mean
    new_weights_ref[number] = weights_ref[number] - LEARN_RATE * grads / (
        jnp.sqrt(accum) + EPSILON
    )
    return accum.T[0:1]


def own_kernel(pieces, core_ref, weights_ref, accum_ref, *rest):
    piece_refs, (new_weights_ref, new_accum_ref, send_ref) = rest[:-3], rest[-3:]
    held = weights_ref.shape[0]
    mine = core_ref[0] == 0
    rows = []
    for t in range(held):
        total = piece_refs[t * pieces][0]
        for piece_ref in piece_refs[t * pieces + 1 : (t + 1) * pieces]:
            total = total + piece_ref[0].astype(F32)
        send_ref[t] = total[1].astype(BF16)
        accum = jnp.where(mine, accum_ref[t : t + 1], accum_ref[held + t : held + t + 1])
        rows.append(adagrad(t, total[0], weights_ref, accum, new_weights_ref))
    new_accum_ref[...] = jnp.concatenate(rows, 0)


def other_kernel(core_ref, weights_ref, accum_ref, grads_ref, own_accum_ref, *rest):
    new_weights_ref, new_accum_ref = rest[-2:]
    held = weights_ref.shape[0]
    mine = core_ref[0] == 0
    rows = []
    for t in range(held):
        accum = jnp.where(mine, accum_ref[held + t : held + t + 1], accum_ref[t : t + 1])
        grads = grads_ref[t].astype(F32)
        rows.append(adagrad(t, grads, weights_ref, accum, new_weights_ref))
    other, own = jnp.concatenate(rows, 0), own_accum_ref[...]
    new_accum_ref[...] = jnp.concatenate(
        [jnp.where(mine, own, other), jnp.where(mine, other, own)], 0
    )


def update(core, weights, accum, staying, pieces):
    tables, words, lanes = weights.shape
    held = tables // CORES
    part = 256
    mine = pl.BlockSpec((held, part, lanes), lambda q, core: (core[0], q, 0))
    others = pl.BlockSpec((held, part, lanes), lambda q, core: (1 - core[0], q, 0))
    moved = pl.BlockSpec((held, part, lanes), lambda q, core: (0, q, 0))
    row = pl.BlockSpec((tables, part), lambda q, core: (0, q))
    half = pl.BlockSpec((held, part), lambda q, core: (0, q))
    flat, specs = [], []
    for t in range(held):
        for n, array in enumerate([staying] + pieces[t]):
            flat.append(array)
            place = 0 if n else t
            specs.append(
                pl.BlockSpec((1, CORES, part, lanes), lambda q, core, n=place: (n, 0, q, 0))
            )
    new_weights, own_accum, send = pl.pallas_call(
        functools.partial(own_kernel, 1 + len(pieces[0])),
        grid_spec=pltpu.PrefetchScalarGridSpec(
            num_scalar_prefetch=1,
            grid=(words // part,),
            in_specs=[mine, row] + specs,
            out_specs=[mine, half, moved],
        ),
        out_shape=[
            jax.ShapeDtypeStruct(weights.shape, F32),
            jax.ShapeDtypeStruct((held, words), F32),
            jax.ShapeDtypeStruct((held, words, lanes), BF16),
        ],
        compiler_params=params(SMALL),
        cost_estimate=cost(3),
    )(core, weights, accum, *flat)
    grads = lax.ppermute(send, "core", [(0, 1), (1, 0)])
    return pl.pallas_call(
        other_kernel,
        grid_spec=pltpu.PrefetchScalarGridSpec(
            num_scalar_prefetch=1,
            grid=(words // part,),
            in_specs=[others, row, moved, half, pl.BlockSpec(memory_space=pl.ANY)],
            out_specs=[others, row],
        ),
        out_shape=[
            jax.ShapeDtypeStruct(weights.shape, F32),
            jax.ShapeDtypeStruct(accum.shape, F32),
        ],
        input_output_aliases={5: 0},
        compiler_params=params(SMALL),
        cost_estimate=cost(2),
    )(core, weights, accum, grads, own_accum, new_weights)


def local(dense_out, pooled, dense_cot, pair_cot, bag_ids, weights, accum):
    samples = dense_out.shape[0]
    tables, slots, _ = bag_ids.shape
    words = weights.shape[1]
    chips = lax.axis_size("chip")
    devices = chips * CORES
    owners = lax.axis_size("wide") * CORES
    held = tables // owners
    core = lax.axis_index("core")
    hst = (lax.axis_index("chip") * CORES + core).reshape(1)

    def spread(x):
        return lax.all_to_all(x, ("wide", "core"), split_axis=0, concat_axis=0, tiled=True)

    late = samples - EARLY
    early_pairs, late_pairs = pair_cot[:EARLY], pair_cot[EARLY:]
    early_dense, send = interact(dense_out, pooled, dense_cot, early_pairs, bag_ids, owners, 0)
    received = spread(send)
    late_dense, send = interact(dense_out, pooled, dense_cot, late_pairs, None, owners, EARLY)
    d_dense = jnp.concatenate([early_dense, late_dense], 0)
    before, counts, own = early_sums(hst, received, held, slots, words, EARLY, late, chips)
    received = spread(send)
    pieces = []
    for t in range(held):
        prior = before if t else in_hbm(before)
        sums = list(row_sums(hst, counts, received, prior, AWAY, t, 1))
        before, sums[0] = lax.optimization_barrier((before, sums[0]))
        moved = []
        for d in AWAY:
            ring = [(i, (i + d) % chips) for i in range(chips)]
            moved.append(lax.ppermute(sums[d - 1], "chip", ring))
        pieces.append(moved)
    before, pieces[0] = lax.optimization_barrier((before, pieces[0]))
    (staying,) = row_sums(hst, own, received, before, (0,), 0, held)
    new_weights, new_accum = update(core.reshape(1), weights, accum, staying, pieces)
    return d_dense, new_weights, new_accum


def solution(mesh):
    hst, wide = mesh.devices.shape
    split = Mesh(mesh.devices.reshape(hst // CORES, CORES, wide), ("chip", "core", "wide"))
    every = ("chip", "core", "wide")
    rows = ("chip", "core")
    in_specs = (
        P(every, None),
        P(every, None),
        P(every, None),
        P(every, None),
        P(None, None, every),
        P("wide", rows, None),
        P("wide", rows),
    )
    out_specs = (P(every, None), P("wide", rows, None), P("wide", rows))
    return jax.shard_map(local, mesh=split, in_specs=in_specs, out_specs=out_specs, check_vma=False)
```

```python
import functools

import jax
import jax.numpy as jnp
from jax import lax
from jax.experimental import pallas as pl
from jax.experimental.pallas import tpu as pltpu
from jax.sharding import Mesh
from jax.sharding import PartitionSpec as P

LEARN_RATE = 0.5
EPSILON = 1e-08
LANES = 128
HALF = 64
FIELD = 4
BLOCK = 32
CORES = 2
CODE = 7
STRIP = 64
VMEM = 40 << 20
FULL = 62 << 20
SMALL = 12 << 20
EARLY = 64
GROUP = 8
AWAY = (1, 2, 3)
BF16 = jnp.bfloat16
F32 = jnp.float32


def cost(micros):
    return pl.CostEstimate(flops=int(micros * 2e8), bytes_accessed=1 << 16, transcendentals=0)


def in_hbm(x):
    return pltpu.with_memory_space_constraint(x, pltpu.HBM)


def params(size=VMEM):
    return pltpu.CompilerParams(vmem_limit_bytes=size)


def encode(ids):
    high = lax.shift_right_logical(ids, CODE)
    value = ((1 << CODE) + (ids & ((1 << CODE) - 1))).astype(F32)
    for bit in range(5):
        value = jnp.where((high >> bit) & 1 == 1, value * 2.0 ** (1 << bit), value)
    return value.astype(BF16)


def decode(codes):
    value = codes.astype(F32)
    high = jnp.zeros(value.shape, jnp.int32)
    for bit in range(4, -1, -1):
        large = value >= 2.0 ** (CODE + (1 << bit))
        value = jnp.where(large, value * 2.0 ** -(1 << bit), value)
        high = jnp.where(large, high + (1 << bit), high)
    return (high << CODE) + value.astype(jnp.int32) - (1 << CODE)


def interact_kernel(steps, with_ids, dense_ref, pooled_ref, cot_ref, pair_ref, *rest):
    if with_ids:
        ids_ref, *rest = rest
    d_dense_ref, send_ref, *scratch = rest
    tables = pooled_ref.shape[1] // LANES
    held = tables // send_ref.shape[0]

    @pl.when(pl.program_id(0) == 0)
    def _():
        for ref in scratch[1:3]:
            ref[...] = jnp.zeros_like(ref)

    if not with_ids:
        interact_block(dense_ref, pooled_ref, cot_ref, pair_ref, d_dense_ref, send_ref, *scratch)
        return

    *scratch, turned = scratch
    pairs = pair_ref.shape[0]

    @pl.when(pl.program_id(0) == 0)
    def _():
        for at in range(0, pairs, LANES):
            end = min(at + LANES, pairs)
            turned[:, at:end] = pair_ref[at:end, :].astype(F32).T

    @pl.when(pl.program_id(0) < steps)
    def _():
        block = pl.ds(pl.multiple_of(pl.program_id(0) * BLOCK, BLOCK), BLOCK)
        block_pairs = turned.at[block, 0:pairs]
        interact_block(dense_ref, pooled_ref, cot_ref, block_pairs, d_dense_ref, send_ref, *scratch)

    @pl.when(pl.program_id(0) == steps)
    def _():
        slots = ids_ref.shape[1]
        for owner in range(tables // held):
            ids = ids_ref[owner * held : (owner + 1) * held]
            send_ref[owner, 0 : held * slots, :] = encode(ids.reshape(held * slots, -1))


def interact_block(
    dense_ref, pooled_ref, cot_ref, pair_ref, d_dense_ref, send_ref, wide_pairs, lower, feats, grads
):
    block = dense_ref.shape[0]
    half = block // 2
    tables = pooled_ref.shape[1] // LANES
    rows = lower.shape[1]

    wide_pairs[:, 0 : pair_ref.shape[1]] = pair_ref[...].astype(F32)
    lane = lax.broadcasted_iota(jnp.int32, (half, LANES), 1)
    for i in range(1, tables + 1):
        start = i * (i - 1) // 2
        base = start // LANES * LANES
        shift = start - base
        to_low = (LANES - shift) % LANES
        to_high = (HALF - shift) % LANES

        def rolled(first, amount, at):
            piece = wide_pairs[first : first + half, at : at + LANES]
            return pltpu.roll(piece, amount, 1) if amount else piece

        low = rolled(0, to_low, base)
        high = rolled(half, to_high, base)
        if shift + i > LANES:
            low = jnp.where(lane < LANES - shift, low, rolled(0, to_low, base + LANES))
            high = jnp.where(
                lane < HALF + LANES - shift, high, rolled(half, to_high, base + LANES)
            )
        if i < HALF:
            low = jnp.where(lane < i, low, 0.0)
            high = jnp.where(lane < HALF + i, high, 0.0)
        lower[:, i, :] = jnp.where(lane < HALF, low, high)

    feats[:, 0, :] = dense_ref[...].astype(F32)
    for t in range(tables):
        feats[:, t + 1, :] = pooled_ref[:, t * LANES : (t + 1) * LANES].astype(F32)

    row_lane = lax.broadcasted_iota(jnp.int32, (rows, LANES), 1)
    below = jnp.zeros((rows - HALF, LANES), F32)

    def two_samples(b, carry):
        both = lower[b]
        turned = both.astype(BF16).T.astype(F32)
        turned = jnp.concatenate([turned, jnp.zeros((LANES, LANES - rows), F32)], 1)
        first = jnp.where(row_lane < HALF, both, 0.0)
        second = jnp.where(row_lane < HALF, pltpu.roll(both, HALF, 1), 0.0)
        first = first + jnp.concatenate([turned[:HALF], below], 0)
        second = second + jnp.concatenate([turned[HALF:], below], 0)
        for pairs, sample in ((first, b), (second, b + half)):
            out = jnp.dot(
                pairs[:, :rows].astype(BF16),
                feats[sample].astype(BF16),
                preferred_element_type=F32,
            )
            grads[:, pl.ds(sample, 1), :] = out.reshape(rows, 1, LANES)
        return carry

    lax.fori_loop(0, half, two_samples, 0, unroll=8)

    d_dense_ref[...] = (grads[0, 0:block] + cot_ref[...].astype(F32)).astype(BF16)
    owners = send_ref.shape[0]
    held = tables // owners
    for t in range(tables):
        place = t % held * LANES
        send_ref[t // held, :, place : place + LANES] = grads[t + 1, 0:block].astype(BF16)


def interact(dense_out, pooled, dense_cot, pair_cot, ids, owners, first, samples):
    tables = pooled.shape[1] // LANES
    pairs = pair_cot.shape[1 if ids is None else 0]
    held = tables // owners
    rows = (tables + 1 + 7) // 8 * 8
    padded = (pairs // LANES + 1) * LANES
    skip, steps = first // BLOCK, samples // BLOCK
    with_ids = ids is not None
    slots = ids.shape[1] if with_ids else 0

    def at(s):
        return (skip + jnp.minimum(s, steps - 1), 0)

    specs = [
        pl.BlockSpec((BLOCK, LANES), at),
        pl.BlockSpec((BLOCK, tables * LANES), at),
        pl.BlockSpec((BLOCK, LANES), at),
        pl.BlockSpec((BLOCK, pairs), lambda s: (jnp.minimum(s, steps - 1), 0)),
    ]
    operands = [in_hbm(x) for x in (dense_out, pooled, dense_cot, pair_cot)]
    scratch = [
        pltpu.VMEM((BLOCK, padded), F32),
        pltpu.VMEM((BLOCK // 2, rows, LANES), F32),
        pltpu.VMEM((BLOCK, rows, LANES), F32),
        pltpu.VMEM((rows, BLOCK + 8, LANES), F32),
    ]
    if with_ids:
        specs[-1] = pl.BlockSpec((pairs, LANES), lambda s: (0, 0))
        scratch.append(pltpu.VMEM((LANES, padded), F32))
        specs.append(pl.BlockSpec(ids.shape, lambda s: (0, 0, 0)))
        operands.append(in_hbm(ids))
    extra = 1 if with_ids else 0
    return pl.pallas_call(
        functools.partial(interact_kernel, steps, with_ids),
        grid=(steps + extra,),
        in_specs=specs,
        out_specs=[
            pl.BlockSpec((BLOCK, LANES), lambda s: (jnp.minimum(s, steps - 1), 0)),
            pl.BlockSpec((owners, BLOCK, held * LANES), lambda s: (0, s, 0)),
        ],
        out_shape=[
            jax.ShapeDtypeStruct((samples, LANES), BF16),
            pltpu.HBM((owners, samples + extra * held * slots, held * LANES), BF16),
        ],
        scratch_shapes=scratch,
        compiler_params=params(FULL),
        cost_estimate=cost(20 * samples / 256),
    )(*operands)


def slot_words(first, samples, words, table, codes_ref):
    sources, rows, _ = codes_ref.shape
    slots = 32 // FIELD
    bits = words.bit_length() - 1
    codes = jnp.concatenate(
        [codes_ref[source, :, first : first + samples] for source in range(sources)], 1
    ).astype(F32)
    mine = codes[:slots]
    for other in range(1, rows // slots):
        mine = jnp.where(table == other, codes[other * slots : (other + 1) * slots], mine)
    ids = decode(mine)
    word = ids & (words - 1)
    one = jnp.left_shift(1, FIELD * lax.shift_right_logical(ids, bits))
    total = one
    for by in range(1, slots):
        total = total + jnp.where(word == pltpu.roll(word, by, 0), pltpu.roll(one, by, 0), 0)
    return word, total


def count_column(word, total, at, out_ref):
    words = out_ref.shape[0]
    slots = word.shape[0]
    place = lax.broadcasted_iota(jnp.int32, (STRIP, LANES), 0)
    words_at = [word[slot : slot + 1, at : at + LANES] for slot in range(slots)]
    totals_at = [total[slot : slot + 1, at : at + LANES] for slot in range(slots)]
    for start in range(0, words, STRIP):
        out = jnp.zeros((STRIP, LANES), jnp.int32)
        for slot in range(slots):
            out = jnp.where(words_at[slot] == place + start, totals_at[slot], out)
        out_ref[start : start + STRIP, at : at + LANES] = out


def early_kernel(late, hst_ref, grads_ref, codes_ref, total_ref, late_ref, own_ref, counts_ref):
    @pl.when(pl.program_id(1) == 0)
    def _():
        total_ref[...] = jnp.zeros_like(total_ref)

    group, samples, _ = grads_ref.shape
    chips = total_ref.shape[1]
    fields = chips * CORES
    words = counts_ref.shape[0]
    table = pl.program_id(0)
    word, total = slot_words(0, samples, words, table, codes_ref)
    for at in range(0, counts_ref.shape[1], LANES):
        count_column(word, total, at, counts_ref)
    grads = grads_ref[...].reshape(group * samples, LANES)
    word, total = slot_words(samples, late, words, table, codes_ref)
    lanes = list(range(0, late_ref.shape[3], LANES))
    here, core = hst_ref[0] // CORES, lax.rem(hst_ref[0], CORES)
    for field in range(fields):
        if field < fields - 1:
            taken, scale = counts_ref[...] & (((1 << FIELD) - 1) << (FIELD * field)), FIELD * field
        else:
            taken, scale = lax.shift_right_logical(counts_ref[...], FIELD * field), 0
        part = jnp.dot(
            taken.astype(F32).astype(BF16), grads, preferred_element_type=F32
        )
        chip = lax.rem(field // CORES + 2 * chips - 1 - here, chips)
        c = lax.rem(field + core, CORES)
        total_ref[0, chip, c] += part * 2.0**-scale
        begin, end = (len(lanes) * n // fields for n in (field, field + 1))
        for at in lanes[begin:end]:
            count_column(word, total, at, late_ref.at[0, 0])
            columns = slice(at, at + LANES)
            for c in range(CORES):
                field = CORES * here + lax.rem(core + c, CORES)
                own = (late_ref[0, 0, :, columns] >> (FIELD * field)) & ((1 << FIELD) - 1)
                own_ref[0, 0, c, :, columns] = own.astype(jnp.int8)


def early_sums(hst, received, held, slots, words, early, late, chips):
    sources, rows, lanes = received.shape
    groups = sources // GROUP
    codes = held * slots
    last = rows // codes - 1
    totals = (chips, CORES, words, LANES)
    return pl.pallas_call(
        functools.partial(early_kernel, late),
        grid_spec=pltpu.PrefetchScalarGridSpec(
            num_scalar_prefetch=1,
            grid=(held, groups),
            in_specs=[
                pl.BlockSpec((GROUP, early, LANES), lambda t, g, hst: (g, 0, t)),
                pl.BlockSpec((GROUP, codes, lanes), lambda t, g, hst: (g, last, 0)),
            ],
            out_specs=[
                pl.BlockSpec((1,) + totals, lambda t, g, hst: (t, 0, 0, 0, 0)),
                pl.BlockSpec((1, 1, words, GROUP * late), lambda t, g, hst: (t, g, 0, 0)),
                pl.BlockSpec((1, 1, CORES, words, GROUP * late), lambda t, g, hst: (t, g, 0, 0, 0)),
            ],
            scratch_shapes=[pltpu.VMEM((words, GROUP * early), jnp.int32)],
        ),
        out_shape=[
            jax.ShapeDtypeStruct((held,) + totals, F32),
            pltpu.HBM((held, groups, words, GROUP * late), jnp.int32),
            pltpu.HBM((held, groups, CORES, words, GROUP * late), jnp.int8),
        ],
        compiler_params=params(FULL),
        cost_estimate=cost(25),
    )(hst, in_hbm(received), in_hbm(received))


def picked(counts, hst_ref, d, c):
    chips = 32 // FIELD // CORES
    here, core = hst_ref[0] // CORES, lax.rem(hst_ref[0], CORES)
    field = CORES * lax.rem(here + d, chips) + lax.rem(core + c, CORES)
    return ((counts >> (FIELD * field)) & ((1 << FIELD) - 1)).astype(F32).astype(BF16)


def sum_kernel(ds, hst_ref, counts_ref, grads_ref, before_ref, *rest):
    outs, total = rest[:-1], rest[-1]

    @pl.when(pl.program_id(1) == 0)
    def _():
        total[...] = before_ref[0]

    group, samples, _ = grads_ref.shape
    grads = grads_ref[...].reshape(group * samples, LANES)
    for k, d in enumerate(ds):
        for c in range(CORES):
            if d:
                counts = picked(counts_ref[0, 0], hst_ref, d, c)
            else:
                counts = counts_ref[0, 0, c].astype(BF16)
            total[k, c] += jnp.dot(counts, grads, preferred_element_type=F32)

    @pl.when(pl.program_id(1) == pl.num_programs(1) - 1)
    def _():
        for k, out in enumerate(outs):
            out[0] = total[k].astype(out.dtype)


def row_sums(hst, counts, grads, before, ds, first, tables):
    groups, words, columns = counts.shape[1], counts.shape[-2], counts.shape[-1]
    group = grads.shape[0] // groups
    samples = columns // group
    at = (ds[0] - 1) % before.shape[1] // len(ds)
    fixed = (0,) * (counts.ndim - 2)
    return pl.pallas_call(
        functools.partial(sum_kernel, ds),
        grid_spec=pltpu.PrefetchScalarGridSpec(
            num_scalar_prefetch=1,
            grid=(tables, groups),
            in_specs=[
                pl.BlockSpec((1, 1) + counts.shape[2:], lambda t, g, hst: (first + t, g) + fixed),
                pl.BlockSpec((group, samples, LANES), lambda t, g, hst: (g, 0, first + t)),
                pl.BlockSpec(
                    (1, len(ds), CORES, words, LANES), lambda t, g, hst: (first + t, at, 0, 0, 0)
                ),
            ],
            out_specs=[
                pl.BlockSpec((1, CORES, words, LANES), lambda t, g, hst: (t, 0, 0, 0)) for d in ds
            ],
            scratch_shapes=[pltpu.VMEM((len(ds), CORES, words, LANES), F32)],
        ),
        out_shape=[
            jax.ShapeDtypeStruct((tables, CORES, words, LANES), BF16 if d else F32) for d in ds
        ],
        compiler_params=params(),
        cost_estimate=cost(0.1),
    )(hst, in_hbm(counts), in_hbm(grads), before)


def adagrad(number, grads, weights_ref, accum, new_weights_ref):
    rows, lanes = grads.shape
    mean = jnp.sum(grads * grads, 1, keepdims=True) * (1.0 / lanes)
    accum = jnp.broadcast_to(accum, (lanes, rows)).T + mean
    new_weights_ref[number] = weights_ref[number] - LEARN_RATE * grads / (
        jnp.sqrt(accum) + EPSILON
    )
    return accum.T[0:1]


def own_kernel(pieces, core_ref, weights_ref, accum_ref, *rest):
    piece_refs, (new_weights_ref, new_accum_ref, send_ref) = rest[:-3], rest[-3:]
    held = weights_ref.shape[0]
    mine = core_ref[0] == 0
    rows = []
    for t in range(held):
        total = piece_refs[t * pieces][0]
        for piece_ref in piece_refs[t * pieces + 1 : (t + 1) * pieces]:
            total = total + piece_ref[0].astype(F32)
        send_ref[t] = total[1].astype(BF16)
        accum = jnp.where(mine, accum_ref[t : t + 1], accum_ref[held + t : held + t + 1])
        rows.append(adagrad(t, total[0], weights_ref, accum, new_weights_ref))
    new_accum_ref[...] = jnp.concatenate(rows, 0)


def other_kernel(core_ref, weights_ref, accum_ref, grads_ref, own_accum_ref, *rest):
    new_weights_ref, new_accum_ref = rest[-2:]
    held = weights_ref.shape[0]
    mine = core_ref[0] == 0
    rows = []
    for t in range(held):
        accum = jnp.where(mine, accum_ref[held + t : held + t + 1], accum_ref[t : t + 1])
        grads = grads_ref[t].astype(F32)
        rows.append(adagrad(t, grads, weights_ref, accum, new_weights_ref))
    other, own = jnp.concatenate(rows, 0), own_accum_ref[...]
    new_accum_ref[...] = jnp.concatenate(
        [jnp.where(mine, own, other), jnp.where(mine, other, own)], 0
    )


def update(core, weights, accum, staying, pieces):
    tables, words, lanes = weights.shape
    held = tables // CORES
    part = 256
    mine = pl.BlockSpec((held, part, lanes), lambda q, core: (core[0], q, 0))
    others = pl.BlockSpec((held, part, lanes), lambda q, core: (1 - core[0], q, 0))
    moved = pl.BlockSpec((held, part, lanes), lambda q, core: (0, q, 0))
    row = pl.BlockSpec((tables, part), lambda q, core: (0, q))
    half = pl.BlockSpec((held, part), lambda q, core: (0, q))
    flat, specs = [], []
    for t in range(held):
        for n, array in enumerate([staying] + pieces[t]):
            flat.append(array)
            place = 0 if n else t
            specs.append(
                pl.BlockSpec((1, CORES, part, lanes), lambda q, core, n=place: (n, 0, q, 0))
            )
    new_weights, own_accum, send = pl.pallas_call(
        functools.partial(own_kernel, 1 + len(pieces[0])),
        grid_spec=pltpu.PrefetchScalarGridSpec(
            num_scalar_prefetch=1,
            grid=(words // part,),
            in_specs=[mine, row] + specs,
            out_specs=[mine, half, moved],
        ),
        out_shape=[
            jax.ShapeDtypeStruct(weights.shape, F32),
            jax.ShapeDtypeStruct((held, words), F32),
            jax.ShapeDtypeStruct((held, words, lanes), BF16),
        ],
        compiler_params=params(SMALL),
        cost_estimate=cost(3),
    )(core, weights, accum, *flat)
    grads = lax.ppermute(send, "core", [(0, 1), (1, 0)])
    return pl.pallas_call(
        other_kernel,
        grid_spec=pltpu.PrefetchScalarGridSpec(
            num_scalar_prefetch=1,
            grid=(words // part,),
            in_specs=[others, row, moved, half, pl.BlockSpec(memory_space=pl.ANY)],
            out_specs=[others, row],
        ),
        out_shape=[
            jax.ShapeDtypeStruct(weights.shape, F32),
            jax.ShapeDtypeStruct(accum.shape, F32),
        ],
        input_output_aliases={5: 0},
        compiler_params=params(SMALL),
        cost_estimate=cost(2),
    )(core, weights, accum, grads, own_accum, new_weights)


def local(dense_out, pooled, dense_cot, pair_cot, bag_ids, weights, accum):
    samples = dense_out.shape[0]
    tables, slots, _ = bag_ids.shape
    words = weights.shape[1]
    chips = lax.axis_size("chip")
    devices = chips * CORES
    owners = lax.axis_size("wide") * CORES
    held = tables // owners
    core = lax.axis_index("core")
    hst = (lax.axis_index("chip") * CORES + core).reshape(1)

    def spread(x):
        return lax.all_to_all(x, ("wide", "core"), split_axis=0, concat_axis=0, tiled=True)

    late = samples - EARLY
    shared = (dense_out, pooled, dense_cot)
    early_dense, send = interact(*shared, pair_cot.T, bag_ids, owners, 0, EARLY)
    received = spread(send)
    late_dense, send = interact(*shared, pair_cot[EARLY:], None, owners, EARLY, late)
    d_dense = jnp.concatenate([early_dense, late_dense], 0)
    before, counts, own = early_sums(hst, received, held, slots, words, EARLY, late, chips)
    received = spread(send)
    pieces = []
    for t in range(held):
        prior = before if t else in_hbm(before)
        sums = list(row_sums(hst, counts, received, prior, AWAY, t, 1))
        before, sums[0] = lax.optimization_barrier((before, sums[0]))
        moved = []
        for d in AWAY:
            ring = [(i, (i + d) % chips) for i in range(chips)]
            moved.append(lax.ppermute(sums[d - 1], "chip", ring))
        pieces.append(moved)
    before, pieces[0] = lax.optimization_barrier((before, pieces[0]))
    (staying,) = row_sums(hst, own, received, before, (0,), 0, held)
    new_weights, new_accum = update(core.reshape(1), weights, accum, staying, pieces)
    return d_dense, new_weights, new_accum


def solution(mesh):
    hst, wide = mesh.devices.shape
    split = Mesh(mesh.devices.reshape(hst // CORES, CORES, wide), ("chip", "core", "wide"))
    every = ("chip", "core", "wide")
    rows = ("chip", "core")
    in_specs = (
        P(every, None),
        P(every, None),
        P(every, None),
        P(every, None),
        P(None, None, every),
        P("wide", rows, None),
        P("wide", rows),
    )
    out_specs = (P(every, None), P("wide", rows, None), P("wide", rows))
    return jax.shard_map(local, mesh=split, in_specs=in_specs, out_specs=out_specs, check_vma=False)
```

```python
import functools

import jax
import jax.numpy as jnp
from jax import lax
from jax.experimental import pallas as pl
from jax.experimental.pallas import tpu as pltpu
from jax.sharding import Mesh
from jax.sharding import PartitionSpec as P

LEARN_RATE = 0.5
EPSILON = 1e-08
LANES = 128
HALF = 64
FIELD = 4
BLOCK = 32
CORES = 2
CODE = 7
STRIP = 64
VMEM = 40 << 20
FULL = 62 << 20
SMALL = 12 << 20
EARLY = 64
GROUP = 8
AWAY = (1, 2, 3)
BF16 = jnp.bfloat16
F32 = jnp.float32


def cost(micros):
    return pl.CostEstimate(flops=int(micros * 2e8), bytes_accessed=1 << 16, transcendentals=0)


def in_hbm(x):
    return pltpu.with_memory_space_constraint(x, pltpu.HBM)


def params(size=VMEM):
    return pltpu.CompilerParams(vmem_limit_bytes=size)


def encode(ids):
    high = lax.shift_right_logical(ids, CODE)
    value = ((1 << CODE) + (ids & ((1 << CODE) - 1))).astype(F32)
    for bit in range(5):
        value = jnp.where((high >> bit) & 1 == 1, value * 2.0 ** (1 << bit), value)
    return value.astype(BF16)


def decode(codes):
    value = codes.astype(F32)
    high = jnp.zeros(value.shape, jnp.int32)
    for bit in range(4, -1, -1):
        large = value >= 2.0 ** (CODE + (1 << bit))
        value = jnp.where(large, value * 2.0 ** -(1 << bit), value)
        high = jnp.where(large, high + (1 << bit), high)
    return (high << CODE) + value.astype(jnp.int32) - (1 << CODE)


def interact_kernel(steps, with_ids, dense_ref, pooled_ref, cot_ref, pair_ref, *rest):
    if with_ids:
        ids_ref, *rest = rest
    d_dense_ref, send_ref, *scratch = rest
    tables = pooled_ref.shape[1] // LANES
    held = tables // send_ref.shape[0]

    @pl.when(pl.program_id(0) == 0)
    def _():
        for ref in scratch[1:3]:
            ref[...] = jnp.zeros_like(ref)

    if not with_ids:
        interact_block(dense_ref, pooled_ref, cot_ref, pair_ref, d_dense_ref, send_ref, *scratch)
        return

    *scratch, turned = scratch
    pairs = pair_ref.shape[0]

    @pl.when(pl.program_id(0) == 0)
    def _():
        for at in range(0, pairs, LANES):
            end = min(at + LANES, pairs)
            turned[:, at:end] = pair_ref[at:end, :].astype(F32).T

    @pl.when(pl.program_id(0) < steps)
    def _():
        block = pl.ds(pl.multiple_of(pl.program_id(0) * BLOCK, BLOCK), BLOCK)
        block_pairs = turned.at[block, 0:pairs]
        interact_block(dense_ref, pooled_ref, cot_ref, block_pairs, d_dense_ref, send_ref, *scratch)

    @pl.when(pl.program_id(0) == steps)
    def _():
        slots = ids_ref.shape[1]
        for owner in range(tables // held):
            ids = ids_ref[owner * held : (owner + 1) * held]
            send_ref[owner, 0 : held * slots, :] = encode(ids.reshape(held * slots, -1))


def interact_block(
    dense_ref, pooled_ref, cot_ref, pair_ref, d_dense_ref, send_ref, wide_pairs, lower, feats, grads
):
    block = dense_ref.shape[0]
    half = block // 2
    tables = pooled_ref.shape[1] // LANES
    rows = lower.shape[1]

    wide_pairs[:, 0 : pair_ref.shape[1]] = pair_ref[...].astype(F32)
    lane = lax.broadcasted_iota(jnp.int32, (half, LANES), 1)
    for i in range(1, tables + 1):
        start = i * (i - 1) // 2
        base = start // LANES * LANES
        shift = start - base
        to_low = (LANES - shift) % LANES
        to_high = (HALF - shift) % LANES

        def rolled(first, amount, at):
            piece = wide_pairs[first : first + half, at : at + LANES]
            return pltpu.roll(piece, amount, 1) if amount else piece

        low = rolled(0, to_low, base)
        high = rolled(half, to_high, base)
        if shift + i > LANES:
            low = jnp.where(lane < LANES - shift, low, rolled(0, to_low, base + LANES))
            high = jnp.where(
                lane < HALF + LANES - shift, high, rolled(half, to_high, base + LANES)
            )
        if i < HALF:
            low = jnp.where(lane < i, low, 0.0)
            high = jnp.where(lane < HALF + i, high, 0.0)
        lower[:, i, :] = jnp.where(lane < HALF, low, high)

    feats[:, 0, :] = dense_ref[...].astype(F32)
    for t in range(tables):
        feats[:, t + 1, :] = pooled_ref[:, t * LANES : (t + 1) * LANES].astype(F32)

    row_lane = lax.broadcasted_iota(jnp.int32, (rows, LANES), 1)
    below = jnp.zeros((rows - HALF, LANES), F32)

    def two_samples(b, carry):
        both = lower[b]
        turned = both.astype(BF16).T.astype(F32)
        turned = jnp.concatenate([turned, jnp.zeros((LANES, LANES - rows), F32)], 1)
        first = jnp.where(row_lane < HALF, both, 0.0)
        second = jnp.where(row_lane < HALF, pltpu.roll(both, HALF, 1), 0.0)
        first = first + jnp.concatenate([turned[:HALF], below], 0)
        second = second + jnp.concatenate([turned[HALF:], below], 0)
        for pairs, sample in ((first, b), (second, b + half)):
            out = jnp.dot(
                pairs[:, :rows].astype(BF16),
                feats[sample].astype(BF16),
                preferred_element_type=F32,
            )
            grads[:, pl.ds(sample, 1), :] = out.reshape(rows, 1, LANES)
        return carry

    lax.fori_loop(0, half, two_samples, 0, unroll=8)

    d_dense_ref[...] = (grads[0, 0:block] + cot_ref[...].astype(F32)).astype(BF16)
    owners = send_ref.shape[0]
    held = tables // owners
    for t in range(tables):
        place = t % held * LANES
        send_ref[t // held, :, place : place + LANES] = grads[t + 1, 0:block].astype(BF16)


def interact(dense_out, pooled, dense_cot, pair_cot, ids, owners, first, samples):
    tables = pooled.shape[1] // LANES
    pairs = pair_cot.shape[1 if ids is None else 0]
    held = tables // owners
    rows = (tables + 1 + 7) // 8 * 8
    padded = (pairs // LANES + 1) * LANES
    skip, steps = first // BLOCK, samples // BLOCK
    with_ids = ids is not None
    slots = ids.shape[1] if with_ids else 0

    def at(s):
        return (skip + jnp.minimum(s, steps - 1), 0)

    specs = [
        pl.BlockSpec((BLOCK, LANES), at),
        pl.BlockSpec((BLOCK, tables * LANES), at),
        pl.BlockSpec((BLOCK, LANES), at),
        pl.BlockSpec((BLOCK, pairs), lambda s: (jnp.minimum(s, steps - 1), 0)),
    ]
    operands = [in_hbm(x) for x in (dense_out, pooled, dense_cot, pair_cot)]
    scratch = [
        pltpu.VMEM((BLOCK, padded), F32),
        pltpu.VMEM((BLOCK // 2, rows, LANES), F32),
        pltpu.VMEM((BLOCK, rows, LANES), F32),
        pltpu.VMEM((rows, BLOCK + 8, LANES), F32),
    ]
    if with_ids:
        specs[-1] = pl.BlockSpec((pairs, LANES), lambda s: (0, 0))
        scratch.append(pltpu.VMEM((LANES, padded), F32))
        specs.append(pl.BlockSpec(ids.shape, lambda s: (0, 0, 0)))
        operands.append(in_hbm(ids))
    extra = 1 if with_ids else 0
    return pl.pallas_call(
        functools.partial(interact_kernel, steps, with_ids),
        grid=(steps + extra,),
        in_specs=specs,
        out_specs=[
            pl.BlockSpec((BLOCK, LANES), lambda s: (jnp.minimum(s, steps - 1), 0)),
            pl.BlockSpec((owners, BLOCK, held * LANES), lambda s: (0, s, 0)),
        ],
        out_shape=[
            jax.ShapeDtypeStruct((samples, LANES), BF16),
            pltpu.HBM((owners, samples + extra * held * slots, held * LANES), BF16),
        ],
        scratch_shapes=scratch,
        compiler_params=params(FULL),
        cost_estimate=cost(20 * samples / 256),
    )(*operands)


def slot_words(first, samples, words, table, codes_ref):
    sources, rows, _ = codes_ref.shape
    slots = 32 // FIELD
    bits = words.bit_length() - 1
    codes = jnp.concatenate(
        [codes_ref[source, :, first : first + samples] for source in range(sources)], 1
    ).astype(F32)
    mine = codes[:slots]
    for other in range(1, rows // slots):
        mine = jnp.where(table == other, codes[other * slots : (other + 1) * slots], mine)
    ids = decode(mine)
    word = ids & (words - 1)
    one = jnp.left_shift(1, FIELD * lax.shift_right_logical(ids, bits))
    total = one
    for by in range(1, slots):
        total = total + jnp.where(word == pltpu.roll(word, by, 0), pltpu.roll(one, by, 0), 0)
    return word, total


def count_column(word, total, at, out_ref):
    words = out_ref.shape[0]
    slots = word.shape[0]
    place = lax.broadcasted_iota(jnp.int32, (STRIP, LANES), 0)
    words_at = [word[slot : slot + 1, at : at + LANES] for slot in range(slots)]
    totals_at = [total[slot : slot + 1, at : at + LANES] for slot in range(slots)]
    for start in range(0, words, STRIP):
        out = jnp.zeros((STRIP, LANES), jnp.int32)
        for slot in range(slots):
            out = jnp.where(words_at[slot] == place + start, totals_at[slot], out)
        out_ref[start : start + STRIP, at : at + LANES] = out


def early_kernel(late, hst_ref, grads_ref, codes_ref, total_ref, late_ref, own_ref, counts_ref):
    @pl.when(pl.program_id(1) == 0)
    def _():
        total_ref[...] = jnp.zeros_like(total_ref)

    group, samples, _ = grads_ref.shape
    chips = total_ref.shape[1]
    fields = chips * CORES
    words = counts_ref.shape[0]
    table = pl.program_id(0)
    word, total = slot_words(0, samples, words, table, codes_ref)
    for at in range(0, counts_ref.shape[1], LANES):
        count_column(word, total, at, counts_ref)
    grads = grads_ref[...].reshape(group * samples, LANES)
    word, total = slot_words(samples, late, words, table, codes_ref)
    lanes = list(range(0, late_ref.shape[3], LANES))
    here, core = hst_ref[0] // CORES, lax.rem(hst_ref[0], CORES)
    for field in range(fields):
        if field < fields - 1:
            taken, scale = counts_ref[...] & (((1 << FIELD) - 1) << (FIELD * field)), FIELD * field
        else:
            taken, scale = lax.shift_right_logical(counts_ref[...], FIELD * field), 0
        part = jnp.dot(
            taken.astype(F32).astype(BF16), grads, preferred_element_type=F32
        )
        chip = lax.rem(field // CORES + 2 * chips - 1 - here, chips)
        c = lax.rem(field + core, CORES)
        total_ref[0, chip, c] += part * 2.0**-scale
        begin, end = (len(lanes) * n // fields for n in (field, field + 1))
        for at in lanes[begin:end]:
            count_column(word, total, at, late_ref.at[0, 0])
            columns = slice(at, at + LANES)
            for c in range(CORES):
                field = CORES * here + lax.rem(core + c, CORES)
                own = (late_ref[0, 0, :, columns] >> (FIELD * field)) & ((1 << FIELD) - 1)
                own_ref[0, 0, c, :, columns] = own.astype(jnp.int8)


def early_sums(hst, received, held, slots, words, early, late, chips):
    sources, rows, lanes = received.shape
    groups = sources // GROUP
    codes = held * slots
    last = rows // codes - 1
    totals = (chips, CORES, words, LANES)
    return pl.pallas_call(
        functools.partial(early_kernel, late),
        grid_spec=pltpu.PrefetchScalarGridSpec(
            num_scalar_prefetch=1,
            grid=(held, groups),
            in_specs=[
                pl.BlockSpec((GROUP, early, LANES), lambda t, g, hst: (g, 0, t)),
                pl.BlockSpec((GROUP, codes, lanes), lambda t, g, hst: (g, last, 0)),
            ],
            out_specs=[
                pl.BlockSpec((1,) + totals, lambda t, g, hst: (t, 0, 0, 0, 0)),
                pl.BlockSpec((1, 1, words, GROUP * late), lambda t, g, hst: (t, g, 0, 0)),
                pl.BlockSpec((1, 1, CORES, words, GROUP * late), lambda t, g, hst: (t, g, 0, 0, 0)),
            ],
            scratch_shapes=[pltpu.VMEM((words, GROUP * early), jnp.int32)],
        ),
        out_shape=[
            jax.ShapeDtypeStruct((held,) + totals, F32),
            pltpu.HBM((held, groups, words, GROUP * late), jnp.int32),
            pltpu.HBM((held, groups, CORES, words, GROUP * late), jnp.int8),
        ],
        compiler_params=params(FULL),
        cost_estimate=cost(25),
    )(hst, in_hbm(received), in_hbm(received))


def picked(counts, hst_ref, d, c):
    chips = 32 // FIELD // CORES
    here, core = hst_ref[0] // CORES, lax.rem(hst_ref[0], CORES)
    field = CORES * lax.rem(here + d, chips) + lax.rem(core + c, CORES)
    return ((counts >> (FIELD * field)) & ((1 << FIELD) - 1)).astype(F32).astype(BF16)


def sum_kernel(ds, hst_ref, counts_ref, grads_ref, before_ref, *rest):
    outs, total = rest[:-1], rest[-1]

    @pl.when(pl.program_id(1) == 0)
    def _():
        total[...] = before_ref[0]

    group, samples, _ = grads_ref.shape
    grads = grads_ref[...].reshape(group * samples, LANES)
    for k, d in enumerate(ds):
        for c in range(CORES):
            if d:
                counts = picked(counts_ref[0, 0], hst_ref, d, c)
            else:
                counts = counts_ref[0, 0, c].astype(BF16)
            total[k, c] += jnp.dot(counts, grads, preferred_element_type=F32)

    @pl.when(pl.program_id(1) == pl.num_programs(1) - 1)
    def _():
        for k, out in enumerate(outs):
            out[0] = total[k].astype(out.dtype)


def row_sums(hst, counts, grads, before, ds, first, tables):
    groups, words, columns = counts.shape[1], counts.shape[-2], counts.shape[-1]
    group = grads.shape[0] // groups
    samples = columns // group
    at = (ds[0] - 1) % before.shape[1] // len(ds)
    fixed = (0,) * (counts.ndim - 2)
    return pl.pallas_call(
        functools.partial(sum_kernel, ds),
        grid_spec=pltpu.PrefetchScalarGridSpec(
            num_scalar_prefetch=1,
            grid=(tables, groups),
            in_specs=[
                pl.BlockSpec((1, 1) + counts.shape[2:], lambda t, g, hst: (first + t, g) + fixed),
                pl.BlockSpec((group, samples, LANES), lambda t, g, hst: (g, 0, first + t)),
                pl.BlockSpec(
                    (1, len(ds), CORES, words, LANES), lambda t, g, hst: (first + t, at, 0, 0, 0)
                ),
            ],
            out_specs=[
                pl.BlockSpec((1, CORES, words, LANES), lambda t, g, hst: (t, 0, 0, 0)) for d in ds
            ],
            scratch_shapes=[pltpu.VMEM((len(ds), CORES, words, LANES), F32)],
        ),
        out_shape=[
            jax.ShapeDtypeStruct((tables, CORES, words, LANES), BF16 if d else F32) for d in ds
        ],
        compiler_params=params(),
        cost_estimate=cost(0.1),
    )(hst, in_hbm(counts), in_hbm(grads), before)


def adagrad(number, grads, weights_ref, accum, new_weights_ref):
    rows, lanes = grads.shape
    mean = jnp.sum(grads * grads, 1, keepdims=True) * (1.0 / lanes)
    accum = jnp.broadcast_to(accum, (lanes, rows)).T + mean
    new_weights_ref[number] = weights_ref[number] - LEARN_RATE * grads / (
        jnp.sqrt(accum) + EPSILON
    )
    return accum.T[0:1]


def own_kernel(pieces, core_ref, weights_ref, accum_ref, *rest):
    piece_refs, (new_weights_ref, new_accum_ref, send_ref) = rest[:-3], rest[-3:]
    held = weights_ref.shape[0]
    mine = core_ref[0] == 0
    rows = []
    for t in range(held):
        total = piece_refs[t * pieces][0]
        for piece_ref in piece_refs[t * pieces + 1 : (t + 1) * pieces]:
            total = total + piece_ref[0].astype(F32)
        send_ref[t] = total[1].astype(BF16)
        accum = jnp.where(mine, accum_ref[t : t + 1], accum_ref[held + t : held + t + 1])
        rows.append(adagrad(t, total[0], weights_ref, accum, new_weights_ref))
    new_accum_ref[...] = jnp.concatenate(rows, 0)


def other_kernel(core_ref, weights_ref, accum_ref, grads_ref, own_accum_ref, *rest):
    new_weights_ref, new_accum_ref = rest[-2:]
    held = weights_ref.shape[0]
    mine = core_ref[0] == 0
    rows = []
    for t in range(held):
        accum = jnp.where(mine, accum_ref[held + t : held + t + 1], accum_ref[t : t + 1])
        grads = grads_ref[t].astype(F32)
        rows.append(adagrad(t, grads, weights_ref, accum, new_weights_ref))
    other, own = jnp.concatenate(rows, 0), own_accum_ref[...]
    new_accum_ref[...] = jnp.concatenate(
        [jnp.where(mine, own, other), jnp.where(mine, other, own)], 0
    )


def update(core, weights, accum, staying, pieces):
    tables, words, lanes = weights.shape
    held = tables // CORES
    part = 512
    mine = pl.BlockSpec((held, part, lanes), lambda q, core: (core[0], q, 0))
    others = pl.BlockSpec((held, part, lanes), lambda q, core: (1 - core[0], q, 0))
    moved = pl.BlockSpec((held, part, lanes), lambda q, core: (0, q, 0))
    row = pl.BlockSpec((tables, part), lambda q, core: (0, q))
    half = pl.BlockSpec((held, part), lambda q, core: (0, q))
    flat, specs = [], []
    for t in range(held):
        for n, array in enumerate([staying] + pieces[t]):
            flat.append(array)
            place = 0 if n else t
            specs.append(
                pl.BlockSpec((1, CORES, part, lanes), lambda q, core, n=place: (n, 0, q, 0))
            )
    new_weights, own_accum, send = pl.pallas_call(
        functools.partial(own_kernel, 1 + len(pieces[0])),
        grid_spec=pltpu.PrefetchScalarGridSpec(
            num_scalar_prefetch=1,
            grid=(words // part,),
            in_specs=[mine, row] + specs,
            out_specs=[mine, half, moved],
        ),
        out_shape=[
            jax.ShapeDtypeStruct(weights.shape, F32),
            jax.ShapeDtypeStruct((held, words), F32),
            jax.ShapeDtypeStruct((held, words, lanes), BF16),
        ],
        compiler_params=params(SMALL),
        cost_estimate=cost(3),
    )(core, weights, accum, *flat)
    grads = lax.ppermute(send, "core", [(0, 1), (1, 0)])
    return pl.pallas_call(
        other_kernel,
        grid_spec=pltpu.PrefetchScalarGridSpec(
            num_scalar_prefetch=1,
            grid=(words // part,),
            in_specs=[others, row, moved, half, pl.BlockSpec(memory_space=pl.ANY)],
            out_specs=[others, row],
        ),
        out_shape=[
            jax.ShapeDtypeStruct(weights.shape, F32),
            jax.ShapeDtypeStruct(accum.shape, F32),
        ],
        input_output_aliases={5: 0},
        compiler_params=params(SMALL),
        cost_estimate=cost(2),
    )(core, weights, accum, grads, own_accum, new_weights)


def local(dense_out, pooled, dense_cot, pair_cot, bag_ids, weights, accum):
    samples = dense_out.shape[0]
    tables, slots, _ = bag_ids.shape
    words = weights.shape[1]
    chips = lax.axis_size("chip")
    devices = chips * CORES
    owners = lax.axis_size("wide") * CORES
    held = tables // owners
    core = lax.axis_index("core")
    hst = (lax.axis_index("chip") * CORES + core).reshape(1)

    def spread(x):
        return lax.all_to_all(x, ("wide", "core"), split_axis=0, concat_axis=0, tiled=True)

    late = samples - EARLY
    shared = (dense_out, pooled, dense_cot)
    early_dense, send = interact(*shared, pair_cot.T, bag_ids, owners, 0, EARLY)
    received = spread(send)
    late_dense, send = interact(*shared, pair_cot[EARLY:], None, owners, EARLY, late)
    d_dense = jnp.concatenate([early_dense, late_dense], 0)
    before, counts, own = early_sums(hst, received, held, slots, words, EARLY, late, chips)
    received = spread(send)
    pieces = []
    for t in range(held):
        prior = before if t else in_hbm(before)
        sums = list(row_sums(hst, counts, received, prior, AWAY, t, 1))
        before, sums[0] = lax.optimization_barrier((before, sums[0]))
        moved = []
        for d in AWAY:
            ring = [(i, (i + d) % chips) for i in range(chips)]
            moved.append(lax.ppermute(sums[d - 1], "chip", ring))
        pieces.append(moved)
    before, pieces[0] = lax.optimization_barrier((before, pieces[0]))
    (staying,) = row_sums(hst, own, received, before, (0,), 0, held)
    new_weights, new_accum = update(core.reshape(1), weights, accum, staying, pieces)
    return d_dense, new_weights, new_accum


def solution(mesh):
    hst, wide = mesh.devices.shape
    split = Mesh(mesh.devices.reshape(hst // CORES, CORES, wide), ("chip", "core", "wide"))
    every = ("chip", "core", "wide")
    rows = ("chip", "core")
    in_specs = (
        P(every, None),
        P(every, None),
        P(every, None),
        P(every, None),
        P(None, None, every),
        P("wide", rows, None),
        P("wide", rows),
    )
    out_specs = (P(every, None), P("wide", rows, None), P("wide", rows))
    return jax.shard_map(local, mesh=split, in_specs=in_specs, out_specs=out_specs, check_vma=False)
```
